32 devices in a mesh: head: 8 (over z, x), blk: 4 (over y, core).
Axes of the slice: x: 2, y: 2, z: 4, core: 2. Of those that a mesh axis runs over, the one named last changes fastest.
Arguments:
- tokens: bfloat16 [8192, 1024], P(('blk', 'head')), may hold values from -6 to 6
- w_proj: bfloat16 [1024, 4096], replicated, may hold values from -0.1875 to 0.1875
- w_out: bfloat16 [1024, 1024], replicated, may hold values from -0.1875 to 0.1875
- cotangent: bfloat16 [8192, 1024], P(('blk', 'head')), may hold values from -6 to 6
- key_blocks: int32 [64, 8], P('blk'), may hold values from 0 to 63, as said below
- exposures: int32 [64, 8], P('blk'), may hold values from 0 to 16, as said below
- positions: int32 [8192], replicated, may hold values from 0 to 4096, as said below
Outputs:
- mixed: bfloat16 [8192, 1024], P(('blk', 'head'))
- grad_u: bfloat16 [1024, 8192], P(None, ('blk', 'head'))
- grad_qkv: float32 [3, 1024, 8192], P(None, 'head', 'blk')
The draws below stay inside these ranges and needn't reach their ends.
Inputs may be any that keep to these rules, and one draw needn't show every extreme that they name: `key_blocks`: every entry is at most its row's index; the first entry of each row is the row's own index; the entries of a row with a nonzero exposure are distinct. `exposures`: the first slot of every row is at least 1; a slot is 0 only in rows with fewer than 8 earlier blocks. `positions`: nondecreasing along the history, starting at 0, rising by 0 or 1 from one event to the next.
All inputs are finite; a program needn't handle non-finite values.
Results may differ from the reference program's by a relative error of at most 0.0083.
Values may be sent and summed in bfloat16 or wider, within the bound.
A program may use at most 128 MiB of HBM per device.

```python
import jax
import jax.numpy as jnp
from jax import lax

HEADS = 32
HEAD_DIM = 32
D = 1024
BLOCK = 128
K_SEL = 8
TOKENS = 8192
BLOCKS = 64
N_BLK = 4


def pattern_common(key):
    rows = jnp.arange(BLOCKS, dtype=jnp.int32)
    cols = rows[None, :]
    scores = jax.random.randint(key, (BLOCKS, BLOCKS), 0, 4096, dtype=jnp.int32)
    distinct = scores * BLOCKS + cols
    ranked = jnp.where(cols < rows[:, None], distinct, -1 - cols)
    ranked = jnp.where(cols == rows[:, None], jnp.int32(2 ** 30), ranked)
    top_values, top_cols = lax.top_k(ranked, K_SEL)
    live = top_values >= 0
    chosen = jnp.where(live, top_cols, rows[:, None])
    return (chosen.astype(jnp.int32), live)


def draw_key_blocks(key, part):
    chosen, live = pattern_common(key)
    return chosen


def draw_exposures(key, part):
    chosen, live = pattern_common(key)
    key = jax.random.fold_in(key, 12)
    counts = jax.random.randint(key, (BLOCKS, K_SEL), 1, 17, dtype=jnp.int32)
    return jnp.where(live, counts, 0).astype(jnp.int32)


def draw_positions(key, part):
    key = jax.random.fold_in(key, 13)
    order = jax.random.permutation(key, jnp.arange(TOKENS - 1, dtype=jnp.int32))
    rises = (order < TOKENS // 2).astype(jnp.int32)
    return jnp.concatenate([jnp.zeros((1,), jnp.int32), jnp.cumsum(rises).astype(jnp.int32)]).astype(jnp.int32)


def steps_of(key, extent, pieces, low, largest):
    def one(dim, blocks):
        heights = jax.random.uniform(jax.random.fold_in(jax.random.fold_in(key, 6), dim), (blocks,), jnp.float32, low / len(pieces), largest / len(pieces))
        return jnp.repeat(jnp.exp(heights), extent[dim] // blocks).reshape((-1,) + (1,) * (len(extent) - dim - 1))

    factor_of = one(*pieces[0])
    for cut in pieces[1:]:
        factor_of = factor_of * one(*cut)
    return factor_of


def gaussian(stream_key, dims, spread, limit, cuts=(), kind=jnp.bfloat16):
    array = spread * jax.random.normal(stream_key, dims, jnp.float32)
    if cuts:
        array = array * steps_of(stream_key, dims, cuts, -0.22, 0.18)
    return jnp.clip(array, -limit, limit).astype(kind)


def setup_inputs(seed: int = 0) -> dict:
    key_list = jax.random.split(jax.random.key(seed), 8)
    tokens = gaussian(key_list[0], (TOKENS, D), 1.0, 6.0, ((0, 32),))
    w_proj = gaussian(key_list[1], (D, 4 * D), D ** -0.5, 0.1875)
    w_out = gaussian(key_list[2], (D, D), D ** -0.5, 0.1875)
    cotangent = gaussian(key_list[3], (TOKENS, D), 1.0, 6.0, ((0, 32),))
    key_blocks = draw_key_blocks(jax.random.fold_in(key_list[7], 71), 0)
    exposures = draw_exposures(jax.random.fold_in(key_list[7], 71), 0)
    positions = draw_positions(jax.random.fold_in(key_list[7], 71), 0)
    return dict(tokens=tokens, w_proj=w_proj, w_out=w_out, cotangent=cotangent, key_blocks=key_blocks, exposures=exposures, positions=positions)


def round_trip(values):
    return lax.optimization_barrier(values.astype(jnp.bfloat16)).astype(jnp.float32)

def silu_slope(values):
    sigmoid = jax.nn.sigmoid(values)
    return sigmoid * (1.0 + values * (1.0 - sigmoid))

def reference(tokens, w_proj, w_out, cotangent, key_blocks, exposures, positions):
    projected = jax.nn.silu(jnp.dot(tokens, w_proj, preferred_element_type=jnp.float32)).astype(jnp.bfloat16)
    gate_u = projected[:, :D].astype(jnp.float32)
    query = projected[:, D:2 * D].reshape(BLOCKS, BLOCK, HEADS, HEAD_DIM)
    keys = projected[:, 2 * D:3 * D].reshape(BLOCKS, BLOCK, HEADS, HEAD_DIM)
    values = projected[:, 3 * D:].reshape(BLOCKS, BLOCK, HEADS, HEAD_DIM)
    weights = jnp.log1p(exposures.astype(jnp.float32))
    pos_blocks = positions.reshape(BLOCKS, BLOCK)
    scaling = HEAD_DIM ** (-0.5)

    def block_terms(row):
        chosen = key_blocks[row]
        query_block = query[row].astype(jnp.float32)
        key_block = keys[chosen].astype(jnp.float32)
        value_block = values[chosen].astype(jnp.float32)
        scores = jnp.einsum('ahe,kbhe->hakb', query_block, key_block) * scaling
        allowed = pos_blocks[chosen][None, None, :, :] <= pos_blocks[row][None, :, None, None]
        coefficient = jnp.where(allowed, weights[row][None, None, :, None], 0.0)
        weighted = round_trip(jax.nn.silu(scores) * coefficient)
        return (chosen, query_block, key_block, value_block, scores, coefficient, weighted)

    def forward_block(row):
        terms = block_terms(row)
        return jnp.einsum('hakb,kbhe->ahe', terms[6], terms[3])
    rows_all = jnp.arange(BLOCKS, dtype=jnp.int32)
    attended = round_trip(lax.map(forward_block, rows_all).reshape(TOKENS, D))
    average = lax.optimization_barrier(jnp.mean(attended, axis=-1, keepdims=True))
    centered = attended - average
    variance = lax.optimization_barrier(jnp.mean(centered * centered, axis=-1, keepdims=True))
    inverse_std = lax.rsqrt(variance + 1e-05)
    normed = centered * inverse_std
    gated = (normed * gate_u).astype(jnp.bfloat16)
    mixed = (tokens.astype(jnp.float32) + jnp.dot(gated, w_out, preferred_element_type=jnp.float32)).astype(jnp.bfloat16)
    d_gated = jnp.dot(cotangent, w_out.T, preferred_element_type=jnp.float32)
    grad_u = (d_gated * normed).astype(jnp.bfloat16).T
    d_normed = d_gated * gate_u
    d_attended = inverse_std * (d_normed - lax.optimization_barrier(jnp.mean(d_normed, axis=-1, keepdims=True)) - normed * lax.optimization_barrier(jnp.mean(d_normed * normed, axis=-1, keepdims=True)))
    d_heads = d_attended.astype(jnp.bfloat16).reshape(BLOCKS, BLOCK, HEADS, HEAD_DIM)

    def backward_block(carry, row):
        grad_keys, grad_values = carry
        chosen, query_block, key_block, value_block, scores, coefficient, weighted = block_terms(row)
        d_block = d_heads[row].astype(jnp.float32)
        d_values = jnp.einsum('hakb,ahe->kbhe', weighted, d_block)
        d_weighted = jnp.einsum('ahe,kbhe->hakb', d_block, value_block)
        d_scores = round_trip(d_weighted * coefficient * silu_slope(scores))
        d_query = jnp.einsum('hakb,kbhe->ahe', d_scores, key_block) * scaling
        d_keys = jnp.einsum('hakb,ahe->kbhe', d_scores, query_block) * scaling
        return ((grad_keys.at[chosen].add(d_keys), grad_values.at[chosen].add(d_values)), d_query)
    per_segment = BLOCKS // N_BLK
    zeros = jnp.zeros((BLOCKS, BLOCK, HEADS, HEAD_DIM), jnp.float32)
    key_total = zeros
    value_total = zeros
    query_parts = []
    for segment in range(N_BLK):
        rows = jnp.arange(segment * per_segment, (segment + 1) * per_segment, dtype=jnp.int32)
        (seg_keys, seg_values), d_query = lax.scan(backward_block, (zeros, zeros), rows)
        key_total = key_total + round_trip(seg_keys)
        value_total = value_total + round_trip(seg_values)
        query_parts.append(d_query)
    grad_query = jnp.concatenate(query_parts, axis=0).reshape(TOKENS, D)
    grad_qkv = jnp.stack([grad_query.T, key_total.reshape(TOKENS, D).T, value_total.reshape(TOKENS, D).T])
    return (mixed, grad_u, grad_qkv)
```

```python
import functools
import math

import jax
import jax.numpy as jnp
from jax import lax
from jax.experimental import pallas as pl
from jax.experimental.pallas import tpu as pltpu
from jax.sharding import PartitionSpec as P

HEADS = 32
HEAD_DIM = 32
BLOCK = 128
SCALING = HEAD_DIM ** (-0.5)
epsilon = 1e-05


def dot_nt(a, b):
    return lax.dot_general(a, b, (((1,), (1,)), ((), ())), preferred_element_type=jnp.float32)


def spread_heads(block, heads):
    head_of = lax.broadcasted_iota(jnp.int32, block.shape, 1) // HEAD_DIM
    return jnp.concatenate(
        [jnp.where(head_of == h, block, jnp.zeros_like(block)) for h in range(heads)], axis=0
    )


def take_heads(wide, heads):
    return jnp.concatenate(
        [
            wide[h * HEAD_DIM : (h + 1) * HEAD_DIM, h * BLOCK : (h + 1) * BLOCK]
            for h in range(heads)
        ],
        axis=0,
    )


def forward_kernel(
    heads, slots, kb_ref, wt_ref, q_ref, kv_ref, posc_ref, posr_ref, o_ref, p_ref, g_ref
):
    i = pl.program_id(0)
    width = q_ref.shape[1]
    q_wide = spread_heads(q_ref[...], heads)
    pair = 2
    out_t = None
    for c in range(slots // pair):
        rows = [
            pl.ds(pl.multiple_of(kb_ref[i * slots + c * pair + s] * BLOCK, BLOCK), BLOCK)
            for s in range(pair)
        ]
        keys = jnp.concatenate([kv_ref[r, :width] for r in rows], axis=0)
        vals = jnp.concatenate([kv_ref[r, width:] for r in rows], axis=0)
        scores = dot_nt(keys, q_wide)
        probs = []
        for s in range(pair):
            weight = wt_ref[i * slots + c * pair + s]
            half = scores[s * BLOCK : (s + 1) * BLOCK, :] * (0.5 * SCALING)
            up = 1.0 + jnp.tanh(half)
            hu = half * up
            slope = up + hu * (2.0 - up)
            if c == 0 and s == 0:
                allowed = posc_ref[...] <= posr_ref[0]
                coefficient = jnp.where(allowed, weight, 0.0)
                coefficient = jnp.concatenate([coefficient] * heads, axis=1)
            else:
                coefficient = weight
            prob = (hu * coefficient).astype(jnp.bfloat16)
            at = (c * pair + s) * BLOCK
            p_ref[0, at : at + BLOCK, :] = prob
            g_ref[0, at : at + BLOCK, :] = (slope * (0.5 * coefficient)).astype(jnp.bfloat16)
            probs.append(prob)
        part = jnp.dot(vals.T, jnp.concatenate(probs, axis=0), preferred_element_type=jnp.float32)
        out_t = part if out_t is None else out_t + part
    o_ref[...] = take_heads(out_t, heads).T.astype(jnp.bfloat16)


def backward_kernel(
    heads, slots, kb_ref, q_ref, do_ref, kv_ref, p_ref, g_ref, dq_ref, dkv_ref, acc_ref
):
    i = pl.program_id(0)
    width = q_ref.shape[1]

    @pl.when(i == 0)
    def _():
        acc_ref[...] = jnp.zeros_like(acc_ref)

    q_wide = spread_heads(q_ref[...], heads)
    do_wide = spread_heads(do_ref[...], heads)
    pair = 2
    dq_t = None
    for c in range(slots // pair):
        rows = [
            pl.ds(pl.multiple_of(kb_ref[i * slots + c * pair + s] * BLOCK, BLOCK), BLOCK)
            for s in range(pair)
        ]
        keys = jnp.concatenate([kv_ref[r, :width] for r in rows], axis=0)
        vals = jnp.concatenate([kv_ref[r, width:] for r in rows], axis=0)
        at = c * pair * BLOCK
        prob = p_ref[0, at : at + pair * BLOCK, :]
        slope = g_ref[0, at : at + pair * BLOCK, :]
        d_scores = (dot_nt(vals, do_wide) * slope.astype(jnp.float32)).astype(jnp.bfloat16)
        d_vals = jnp.dot(prob, do_wide, preferred_element_type=jnp.float32)
        d_keys = jnp.dot(d_scores, q_wide, preferred_element_type=jnp.float32)
        part = jnp.dot(keys.T, d_scores, preferred_element_type=jnp.float32)
        dq_t = part if dq_t is None else dq_t + part
        for s in range(pair):
            acc_ref[rows[s], :width] += d_keys[s * BLOCK : (s + 1) * BLOCK, :]
            acc_ref[rows[s], width:] += d_vals[s * BLOCK : (s + 1) * BLOCK, :]
    dq_ref[...] = take_heads(dq_t, heads) * SCALING

    @pl.when(i == pl.num_programs(0) - 1)
    def _():
        dkv_ref[:, :width] = (acc_ref[:, :width] * SCALING).astype(jnp.bfloat16)
        dkv_ref[:, width:] = acc_ref[:, width:].astype(jnp.bfloat16)


def attention_forward(key_blocks, weights, query, key_vals, positions_here):
    local_blocks, slots = key_blocks.shape
    width = query.shape[1]
    heads = width // HEAD_DIM
    wide = heads * BLOCK
    whole = pl.BlockSpec(memory_space=pltpu.VMEM)
    smem = pl.BlockSpec(memory_space=pltpu.SMEM)
    stored = jax.ShapeDtypeStruct((local_blocks, slots * BLOCK, wide), jnp.bfloat16)
    return pl.pallas_call(
        functools.partial(forward_kernel, heads, slots),
        grid=(local_blocks,),
        in_specs=[
            smem,
            smem,
            pl.BlockSpec((BLOCK, width), lambda i: (i, 0)),
            whole,
            pl.BlockSpec((BLOCK, 1), lambda i: (i, 0)),
            pl.BlockSpec((1, 1, BLOCK), lambda i: (i, 0, 0)),
        ],
        out_specs=[
            pl.BlockSpec((BLOCK, width), lambda i: (i, 0)),
            pl.BlockSpec((1, slots * BLOCK, wide), lambda i: (i, 0, 0)),
            pl.BlockSpec((1, slots * BLOCK, wide), lambda i: (i, 0, 0)),
        ],
        out_shape=[jax.ShapeDtypeStruct(query.shape, jnp.bfloat16), stored, stored],
        compiler_params=pltpu.CompilerParams(vmem_limit_bytes=48 * 1024 * 1024),
        name="attention_forward",
    )(
        key_blocks.reshape(-1),
        weights.reshape(-1),
        query,
        key_vals,
        positions_here.reshape(-1, 1),
        positions_here.reshape(local_blocks, 1, BLOCK),
    )


def attention_backward(key_blocks, query, d_attended, key_vals, prob, slope):
    local_blocks, slots = key_blocks.shape
    width = query.shape[1]
    heads = width // HEAD_DIM
    wide = heads * BLOCK
    total = key_vals.shape[0]
    whole = pl.BlockSpec(memory_space=pltpu.VMEM)
    smem = pl.BlockSpec(memory_space=pltpu.SMEM)
    block = pl.BlockSpec((BLOCK, width), lambda i: (i, 0))
    stored = pl.BlockSpec((1, slots * BLOCK, wide), lambda i: (i, 0, 0))
    return pl.pallas_call(
        functools.partial(backward_kernel, heads, slots),
        grid=(local_blocks,),
        in_specs=[smem, block, block, whole, stored, stored],
        out_specs=[pl.BlockSpec((width, BLOCK), lambda i: (0, i)), whole],
        out_shape=[
            jax.ShapeDtypeStruct((width, query.shape[0]), jnp.float32),
            jax.ShapeDtypeStruct((total, 2 * width), jnp.bfloat16),
        ],
        scratch_shapes=[pltpu.VMEM((total, 2 * width), jnp.float32)],
        compiler_params=pltpu.CompilerParams(vmem_limit_bytes=48 * 1024 * 1024),
        name="attention_backward",
    )(key_blocks.reshape(-1), query, d_attended, key_vals, prob, slope)


def shards(tokens, w_proj, w_out, cotangent, key_blocks, exposures, positions):
    head_count = lax.axis_size("head")
    group_count = lax.axis_size("blk")
    segment_index = lax.axis_index("blk")
    local_rows, width = tokens.shape
    features = width // head_count
    segment = local_rows * head_count
    total_rows = segment * group_count
    projected = jax.nn.silu(
        jnp.dot(tokens, w_proj, preferred_element_type=jnp.float32)
    ).astype(jnp.bfloat16)
    gate_u = projected[:, :width].astype(jnp.float32)
    qkv = projected[:, width:].reshape(local_rows, 3, head_count, features)
    qkv = jnp.transpose(qkv, (2, 1, 0, 3))
    by_head = lax.all_to_all(qkv, "head", split_axis=0, concat_axis=0, tiled=True)
    query = by_head[:, 0].reshape(segment, features)
    key_vals = jnp.concatenate(
        [by_head[:, s].reshape(segment, features) for s in (1, 2)], axis=1
    )
    key_all = lax.all_gather(key_vals, "blk", axis=0, tiled=True)
    positions_here = lax.dynamic_slice_in_dim(positions, segment_index * segment, segment, 0)
    weights = jnp.log1p(exposures.astype(jnp.float32))
    attended, prob, slope = attention_forward(
        key_blocks, weights, query, key_all, positions_here
    )
    by_token = lax.all_to_all(attended, "head", split_axis=0, concat_axis=1, tiled=True)
    by_token = by_token.astype(jnp.float32)
    average = jnp.mean(by_token, axis=1, keepdims=True)
    centered = by_token - average
    variance = jnp.mean(centered * centered, axis=1, keepdims=True)
    inverse_std = lax.rsqrt(variance + epsilon)
    normed = centered * inverse_std
    gated = (normed * gate_u).astype(jnp.bfloat16)
    mixed = (
        tokens.astype(jnp.float32) + jnp.dot(gated, w_out, preferred_element_type=jnp.float32)
    ).astype(jnp.bfloat16)
    d_gated = dot_nt(cotangent, w_out)
    grad_u = (d_gated * normed).astype(jnp.bfloat16).T
    d_normed = d_gated * gate_u
    d_attended = inverse_std * (
        d_normed
        - jnp.mean(d_normed, axis=1, keepdims=True)
        - normed * jnp.mean(d_normed * normed, axis=1, keepdims=True)
    )
    d_heads = lax.all_to_all(
        d_attended.astype(jnp.bfloat16), "head", split_axis=1, concat_axis=0, tiled=True
    )
    grad_query, partial = attention_backward(
        key_blocks, query, d_heads, key_all, prob, slope
    )
    summed = lax.psum_scatter(partial, "blk", scatter_dimension=0, tiled=True)
    summed = summed.T.reshape(2, features, segment).astype(jnp.float32)
    grad_qkv = jnp.concatenate([grad_query[None], summed], axis=0)
    return (mixed, grad_u, grad_qkv)


def solution(mesh):
    in_specs = (
        P(("blk", "head"), None),
        P(),
        P(),
        P(("blk", "head"), None),
        P("blk", None),
        P("blk", None),
        P(),
    )
    out_specs = (P(("blk", "head"), None), P(None, ("blk", "head")), P(None, "head", "blk"))
    return jax.shard_map(shards, mesh=mesh, in_specs=in_specs, out_specs=out_specs, check_vma=False)
```

```python
import functools

import jax
import jax.numpy as jnp
from jax import lax
from jax.experimental import pallas as pl
from jax.experimental.pallas import tpu as pltpu
from jax.sharding import PartitionSpec as P

HEADS = 32
HEAD_DIM = 32
BLOCK = 128
SCALING = HEAD_DIM ** (-0.5)
epsilon = 1e-05


def dot_nt(a, b):
    return lax.dot_general(a, b, (((1,), (1,)), ((), ())), preferred_element_type=jnp.float32)


def spread_heads(block, heads):
    head_of = lax.broadcasted_iota(jnp.int32, block.shape, 1) // HEAD_DIM
    return jnp.concatenate(
        [jnp.where(head_of == h, block, jnp.zeros_like(block)) for h in range(heads)], axis=0
    )


def take_heads(wide, heads):
    return jnp.concatenate(
        [
            wide[h * HEAD_DIM : (h + 1) * HEAD_DIM, h * BLOCK : (h + 1) * BLOCK]
            for h in range(heads)
        ],
        axis=0,
    )


def forward_kernel(
    heads, slots, kb_ref, wt_ref, q_ref, kv_ref, posc_ref, posr_ref, o_ref, p_ref, g_ref
):
    i = pl.program_id(0)
    width = q_ref.shape[1]
    q_wide = spread_heads(q_ref[...], heads)
    pair = 2
    out_t = None
    for c in range(slots // pair):
        rows = [
            pl.ds(pl.multiple_of(kb_ref[i * slots + c * pair + s] * BLOCK, BLOCK), BLOCK)
            for s in range(pair)
        ]
        keys = jnp.concatenate([kv_ref[r, :width] for r in rows], axis=0)
        vals = jnp.concatenate([kv_ref[r, width:] for r in rows], axis=0)
        scores = dot_nt(keys, q_wide)
        probs = []
        for s in range(pair):
            weight = wt_ref[i * slots + c * pair + s]
            half = scores[s * BLOCK : (s + 1) * BLOCK, :] * (0.5 * SCALING)
            up = 1.0 + jnp.tanh(half)
            hu = half * up
            slope = up + hu * (2.0 - up)
            if c == 0 and s == 0:
                allowed = posc_ref[...] <= posr_ref[0]
                coefficient = jnp.where(allowed, weight, 0.0)
                coefficient = jnp.concatenate([coefficient] * heads, axis=1)
            else:
                coefficient = weight
            prob = (hu * coefficient).astype(jnp.bfloat16)
            at = (c * pair + s) * BLOCK
            p_ref[0, at : at + BLOCK, :] = prob
            g_ref[0, at : at + BLOCK, :] = (slope * (0.5 * coefficient)).astype(jnp.bfloat16)
            probs.append(prob)
        part = jnp.dot(vals.T, jnp.concatenate(probs, axis=0), preferred_element_type=jnp.float32)
        out_t = part if out_t is None else out_t + part
    o_ref[...] = take_heads(out_t, heads).T.astype(jnp.bfloat16)


def backward_kernel(
    heads, slots, kb_ref, q_ref, do_ref, kv_ref, p_ref, g_ref, dq_ref, dkv_ref, acc_ref
):
    i = pl.program_id(0)
    width = q_ref.shape[1]

    @pl.when(i == 0)
    def _():
        acc_ref[...] = jnp.zeros_like(acc_ref)

    q_wide = spread_heads(q_ref[...], heads)
    do_wide = spread_heads(do_ref[...], heads)
    pair = 2
    dq_t = None
    for c in range(slots // pair):
        rows = [
            pl.ds(pl.multiple_of(kb_ref[i * slots + c * pair + s] * BLOCK, BLOCK), BLOCK)
            for s in range(pair)
        ]
        keys = jnp.concatenate([kv_ref[r, :width] for r in rows], axis=0)
        vals = jnp.concatenate([kv_ref[r, width:] for r in rows], axis=0)
        at = c * pair * BLOCK
        prob = p_ref[0, at : at + pair * BLOCK, :]
        slope = g_ref[0, at : at + pair * BLOCK, :]
        d_scores = (dot_nt(vals, do_wide) * slope.astype(jnp.float32)).astype(jnp.bfloat16)
        d_vals = jnp.dot(prob, do_wide, preferred_element_type=jnp.float32)
        d_keys = jnp.dot(d_scores, q_wide, preferred_element_type=jnp.float32)
        part = jnp.dot(keys.T, d_scores, preferred_element_type=jnp.float32)
        dq_t = part if dq_t is None else dq_t + part
        for s in range(pair):
            acc_ref[rows[s], :width] += d_keys[s * BLOCK : (s + 1) * BLOCK, :]
            acc_ref[rows[s], width:] += d_vals[s * BLOCK : (s + 1) * BLOCK, :]
    dq_ref[...] = take_heads(dq_t, heads) * SCALING

    @pl.when(i == pl.num_programs(0) - 1)
    def _():
        dkv_ref[:, :width] = (acc_ref[:, :width] * SCALING).astype(jnp.bfloat16)
        dkv_ref[:, width:] = acc_ref[:, width:].astype(jnp.bfloat16)


def attention_forward(key_blocks, weights, query, key_vals, positions_here):
    local_blocks, slots = key_blocks.shape
    width = query.shape[1]
    heads = width // HEAD_DIM
    wide = heads * BLOCK
    whole = pl.BlockSpec(memory_space=pltpu.VMEM)
    smem = pl.BlockSpec(memory_space=pltpu.SMEM)
    stored = jax.ShapeDtypeStruct((local_blocks, slots * BLOCK, wide), jnp.bfloat16)
    return pl.pallas_call(
        functools.partial(forward_kernel, heads, slots),
        grid=(local_blocks,),
        in_specs=[
            smem,
            smem,
            pl.BlockSpec((BLOCK, width), lambda i: (i, 0)),
            whole,
            pl.BlockSpec((BLOCK, 1), lambda i: (i, 0)),
            pl.BlockSpec((1, 1, BLOCK), lambda i: (i, 0, 0)),
        ],
        out_specs=[
            pl.BlockSpec((BLOCK, width), lambda i: (i, 0)),
            pl.BlockSpec((1, slots * BLOCK, wide), lambda i: (i, 0, 0)),
            pl.BlockSpec((1, slots * BLOCK, wide), lambda i: (i, 0, 0)),
        ],
        out_shape=[jax.ShapeDtypeStruct(query.shape, jnp.bfloat16), stored, stored],
        compiler_params=pltpu.CompilerParams(vmem_limit_bytes=48 * 1024 * 1024),
        name="attention_forward",
    )(
        key_blocks.reshape(-1),
        weights.reshape(-1),
        query,
        key_vals,
        positions_here.reshape(-1, 1),
        positions_here.reshape(local_blocks, 1, BLOCK),
    )


def attention_backward(key_blocks, query, d_attended, key_vals, prob, slope):
    local_blocks, slots = key_blocks.shape
    width = query.shape[1]
    heads = width // HEAD_DIM
    wide = heads * BLOCK
    total = key_vals.shape[0]
    whole = pl.BlockSpec(memory_space=pltpu.VMEM)
    smem = pl.BlockSpec(memory_space=pltpu.SMEM)
    block = pl.BlockSpec((BLOCK, width), lambda i: (i, 0))
    stored = pl.BlockSpec((1, slots * BLOCK, wide), lambda i: (i, 0, 0))
    return pl.pallas_call(
        functools.partial(backward_kernel, heads, slots),
        grid=(local_blocks,),
        in_specs=[smem, block, block, whole, stored, stored],
        out_specs=[pl.BlockSpec((width, BLOCK), lambda i: (0, i)), whole],
        out_shape=[
            jax.ShapeDtypeStruct((width, query.shape[0]), jnp.float32),
            jax.ShapeDtypeStruct((total, 2 * width), jnp.bfloat16),
        ],
        scratch_shapes=[pltpu.VMEM((total, 2 * width), jnp.float32)],
        compiler_params=pltpu.CompilerParams(vmem_limit_bytes=48 * 1024 * 1024),
        name="attention_backward",
    )(key_blocks.reshape(-1), query, d_attended, key_vals, prob, slope)


def greet(peers):
    barrier = pltpu.get_barrier_semaphore()
    for peer in peers:
        pl.semaphore_signal(
            barrier, inc=1, device_id=peer, device_id_type=pl.DeviceIdType.MESH
        )
    pl.semaphore_wait(barrier, len(peers))


def send(source, target, send_sem, recv_sem, peer):
    copy = pltpu.make_async_remote_copy(
        src_ref=source,
        dst_ref=target,
        send_sem=send_sem,
        recv_sem=recv_sem,
        device_id=peer,
        device_id_type=pl.DeviceIdType.MESH,
    )
    copy.start()
    return copy


def blk_partners(here):
    return here + 1 - 2 * lax.rem(here, 2), lax.rem(here + 2, 4)


def exchange_kernel(count, x_ref, o_ref, local_sem, send_sem, recv_sem):
    me = lax.axis_index("head")
    others = [lax.rem(me + k, count) for k in range(1, count)]
    greet([{"head": other} for other in others])
    local = pltpu.make_async_copy(x_ref.at[me], o_ref.at[me], local_sem)
    local.start()
    copies = [
        send(x_ref.at[other], o_ref.at[me], send_sem.at[k], recv_sem.at[k], {"head": other})
        for k, other in enumerate(others)
    ]
    local.wait()
    for copy in copies:
        copy.wait()


def exchange(x, collective_id):
    count = x.shape[0]
    anywhere = pl.BlockSpec(memory_space=pl.ANY)
    return pl.pallas_call(
        functools.partial(exchange_kernel, count),
        in_specs=[anywhere],
        out_specs=anywhere,
        out_shape=jax.ShapeDtypeStruct(x.shape, x.dtype),
        scratch_shapes=[
            pltpu.SemaphoreType.DMA,
            pltpu.SemaphoreType.DMA((count - 1,)),
            pltpu.SemaphoreType.DMA((count - 1,)),
        ],
        compiler_params=pltpu.CompilerParams(collective_id=collective_id, has_side_effects=True),
        name="exchange",
    )(x)


def distribute_kernel(
    count, kv_ref, q_ref, kv_out, q_out, local_sem, kv_sem, q_sem, side_sem, core_sem, pass_sem
):
    me, here = lax.axis_index("head"), lax.axis_index("blk")
    core, side = blk_partners(here)
    rows = kv_ref.shape[1]
    others = [lax.rem(me + k, count) for k in range(1, count)]
    greet([{"head": other} for other in others] + [{"blk": core}, {"blk": side}])

    def place(segment, source):
        start = pl.multiple_of((segment * count + source) * rows, rows)
        return kv_out.at[pl.ds(start, rows), :]

    local_kv = pltpu.make_async_copy(kv_ref.at[me], place(here, me), local_sem.at[0])
    local_kv.start()
    local_q = pltpu.make_async_copy(q_ref.at[me], q_out.at[me], local_sem.at[1])
    local_q.start()
    kv_copies = [
        send(
            kv_ref.at[other],
            place(here, me),
            kv_sem.at[0, k],
            kv_sem.at[1, k],
            {"head": other},
        )
        for k, other in enumerate(others)
    ]
    q_copies = [
        send(q_ref.at[other], q_out.at[me], q_sem.at[0, k], q_sem.at[1, k], {"head": other})
        for k, other in enumerate(others)
    ]
    side_copies, core_copies, pass_copies = [], [], []
    lag = 2
    for k in range(count + lag):
        if k < count:
            if k == 0:
                local_kv.wait()
            else:
                kv_copies[k - 1].wait_recv()
            chunk = place(here, lax.rem(me - k + count, count))
            side_copies.append(
                send(chunk, chunk, side_sem.at[0, k], side_sem.at[1, k], {"blk": side})
            )
            core_copies.append(
                send(chunk, chunk, core_sem.at[0, k], core_sem.at[1, k], {"blk": core})
            )
        j = k - lag
        if j >= 0:
            side_copies[j].wait_recv()
            chunk = place(side, lax.rem(me - j + count, count))
            pass_copies.append(
                send(chunk, chunk, pass_sem.at[0, j], pass_sem.at[1, j], {"blk": core})
            )
    local_q.wait()
    for copy in kv_copies + side_copies:
        copy.wait_send()
    for copy in q_copies + core_copies + pass_copies:
        copy.wait()


def distribute(kv, q, groups):
    count, rows, width = kv.shape
    anywhere = pl.BlockSpec(memory_space=pl.ANY)
    pair = pltpu.SemaphoreType.DMA((2, count))
    return pl.pallas_call(
        functools.partial(distribute_kernel, count),
        in_specs=[anywhere, anywhere],
        out_specs=[anywhere, anywhere],
        out_shape=[
            jax.ShapeDtypeStruct((groups * count * rows, width), kv.dtype),
            jax.ShapeDtypeStruct(q.shape, q.dtype),
        ],
        scratch_shapes=[pltpu.SemaphoreType.DMA((2,)), pair, pair, pair, pair, pair],
        compiler_params=pltpu.CompilerParams(collective_id=0, has_side_effects=True),
        name="distribute",
    )(kv, q)


def collect_kernel(
    chunks, part_ref, dq_ref, o_ref, core_in, side_out, side_in, near_sem, far_sem, side_sem
):
    here = lax.axis_index("blk")
    core, side = blk_partners(here)
    far = lax.rem(core + 2, 4)
    width, segment = dq_ref.shape
    rows = segment // chunks
    greet([{"blk": core}, {"blk": side}])
    far_copies = [
        send(
            part_ref.at[far, c], core_in.at[1, c], far_sem.at[0, c], far_sem.at[1, c], {"blk": core}
        )
        for c in range(chunks)
    ]
    near_copies = [
        send(
            part_ref.at[core, c],
            core_in.at[0, c],
            near_sem.at[0, c],
            near_sem.at[1, c],
            {"blk": core},
        )
        for c in range(chunks)
    ]
    side_copies = []
    for c in range(chunks):
        far_copies[c].wait_recv()
        total = part_ref[side, c].astype(jnp.float32) + core_in[1, c].astype(jnp.float32)
        side_out[c] = total.astype(jnp.bfloat16)
        side_copies.append(
            send(
                side_out.at[c], side_in.at[c], side_sem.at[0, c], side_sem.at[1, c], {"blk": side}
            )
        )
    o_ref[:width, :] = dq_ref[...]
    for c in range(chunks):
        near_copies[c].wait_recv()
        side_copies[c].wait_recv()
        total = (
            part_ref[here, c].astype(jnp.float32)
            + core_in[0, c].astype(jnp.float32)
            + side_in[c].astype(jnp.float32)
        )
        o_ref[width:, c * rows : (c + 1) * rows] = total.T
    for copy in far_copies + near_copies + side_copies:
        copy.wait_send()


def collect(partial, grad_query, groups):
    width, segment = grad_query.shape
    chunks = 8
    rows = segment // chunks
    vmem = pl.BlockSpec(memory_space=pltpu.VMEM)
    pair = pltpu.SemaphoreType.DMA((2, chunks))
    block = (chunks, rows, 2 * width)
    return pl.pallas_call(
        functools.partial(collect_kernel, chunks),
        in_specs=[vmem, vmem],
        out_specs=vmem,
        out_shape=jax.ShapeDtypeStruct((3 * width, segment), jnp.float32),
        scratch_shapes=[
            pltpu.VMEM((2,) + block, jnp.bfloat16),
            pltpu.VMEM(block, jnp.bfloat16),
            pltpu.VMEM(block, jnp.bfloat16),
            pair,
            pair,
            pair,
        ],
        compiler_params=pltpu.CompilerParams(
            collective_id=3, has_side_effects=True, vmem_limit_bytes=48 * 1024 * 1024
        ),
        name="collect",
    )(partial.reshape((groups,) + block), grad_query)


def shards(tokens, w_proj, w_out, cotangent, key_blocks, exposures, positions):
    head_count = lax.axis_size("head")
    group_count = lax.axis_size("blk")
    segment_index = lax.axis_index("blk")
    local_rows, width = tokens.shape
    features = width // head_count
    segment = local_rows * head_count
    projected = jax.nn.silu(
        jnp.dot(tokens, w_proj, preferred_element_type=jnp.float32)
    ).astype(jnp.bfloat16)
    gate_u = projected[:, :width].astype(jnp.float32)
    by_owner = projected[:, width:].reshape(local_rows, 3, head_count, features)
    key_vals = jnp.concatenate([by_owner[:, 1], by_owner[:, 2]], axis=2)
    key_all, query = distribute(
        jnp.transpose(key_vals, (1, 0, 2)),
        jnp.transpose(by_owner[:, 0], (1, 0, 2)),
        group_count,
    )
    query = query.reshape(segment, features)
    positions_here = lax.dynamic_slice_in_dim(positions, segment_index * segment, segment, 0)
    weights = jnp.log1p(exposures.astype(jnp.float32))
    attended, prob, slope = attention_forward(
        key_blocks, weights, query, key_all, positions_here
    )
    by_token = exchange(attended.reshape(head_count, local_rows, features), 1)
    by_token = jnp.transpose(by_token, (1, 0, 2)).reshape(local_rows, width)
    by_token = by_token.astype(jnp.float32)
    average = jnp.mean(by_token, axis=1, keepdims=True)
    centered = by_token - average
    variance = jnp.mean(centered * centered, axis=1, keepdims=True)
    inverse_std = lax.rsqrt(variance + epsilon)
    normed = centered * inverse_std
    gated = (normed * gate_u).astype(jnp.bfloat16)
    mixed = (
        tokens.astype(jnp.float32) + jnp.dot(gated, w_out, preferred_element_type=jnp.float32)
    ).astype(jnp.bfloat16)
    d_gated = dot_nt(cotangent, w_out)
    grad_u = (d_gated * normed).astype(jnp.bfloat16).T
    d_normed = d_gated * gate_u
    d_attended = inverse_std * (
        d_normed
        - jnp.mean(d_normed, axis=1, keepdims=True)
        - normed * jnp.mean(d_normed * normed, axis=1, keepdims=True)
    )
    d_attended = d_attended.astype(jnp.bfloat16).reshape(local_rows, head_count, features)
    d_heads = exchange(jnp.transpose(d_attended, (1, 0, 2)), 2).reshape(segment, features)
    grad_query, partial = attention_backward(
        key_blocks, query, d_heads, key_all, prob, slope
    )
    grad_qkv = collect(partial, grad_query, group_count).reshape(3, features, segment)
    return (mixed, grad_u, grad_qkv)


def solution(mesh):
    in_specs = (
        P(("blk", "head"), None),
        P(),
        P(),
        P(("blk", "head"), None),
        P("blk", None),
        P("blk", None),
        P(),
    )
    out_specs = (P(("blk", "head"), None), P(None, ("blk", "head")), P(None, "head", "blk"))
    return jax.shard_map(shards, mesh=mesh, in_specs=in_specs, out_specs=out_specs, check_vma=False)
```

```python
import functools

import jax
import jax.numpy as jnp
from jax import lax
from jax.experimental import pallas as pl
from jax.experimental.pallas import tpu as pltpu
from jax.sharding import PartitionSpec as P

HEADS = 32
HEAD_DIM = 32
BLOCK = 128
SCALING = HEAD_DIM ** (-0.5)
epsilon = 1e-05


def dot_nt(a, b):
    return lax.dot_general(a, b, (((1,), (1,)), ((), ())), preferred_element_type=jnp.float32)


def spread_heads(block, heads):
    head_of = lax.broadcasted_iota(jnp.int32, block.shape, 1) // HEAD_DIM
    return jnp.concatenate(
        [jnp.where(head_of == h, block, jnp.zeros_like(block)) for h in range(heads)], axis=0
    )


def take_heads(wide, heads):
    return jnp.concatenate(
        [
            wide[h * HEAD_DIM : (h + 1) * HEAD_DIM, h * BLOCK : (h + 1) * BLOCK]
            for h in range(heads)
        ],
        axis=0,
    )


def forward_kernel(
    heads, slots, kb_ref, wt_ref, q_ref, kv_ref, posc_ref, posr_ref, o_ref, p_ref, g_ref
):
    i = pl.program_id(0)
    width = q_ref.shape[1]
    q_wide = spread_heads(q_ref[...], heads)
    pair = 2
    out_t = None
    for c in range(slots // pair):
        rows = [
            pl.ds(pl.multiple_of(kb_ref[i * slots + c * pair + s] * BLOCK, BLOCK), BLOCK)
            for s in range(pair)
        ]
        keys = jnp.concatenate([kv_ref[r, :width] for r in rows], axis=0)
        vals = jnp.concatenate([kv_ref[r, width:] for r in rows], axis=0)
        scores = dot_nt(keys, q_wide)
        probs = []
        for s in range(pair):
            weight = wt_ref[i * slots + c * pair + s]
            half = scores[s * BLOCK : (s + 1) * BLOCK, :] * (0.5 * SCALING)
            up = 1.0 + jnp.tanh(half)
            hu = half * up
            slope = up + hu * (2.0 - up)
            if c == 0 and s == 0:
                allowed = posc_ref[...] <= posr_ref[0]
                coefficient = jnp.where(allowed, weight, 0.0)
                coefficient = jnp.concatenate([coefficient] * heads, axis=1)
            else:
                coefficient = weight
            prob = (hu * coefficient).astype(jnp.bfloat16)
            at = (c * pair + s) * BLOCK
            p_ref[0, at : at + BLOCK, :] = prob
            g_ref[0, at : at + BLOCK, :] = (slope * (0.5 * coefficient)).astype(jnp.bfloat16)
            probs.append(prob)
        part = jnp.dot(vals.T, jnp.concatenate(probs, axis=0), preferred_element_type=jnp.float32)
        out_t = part if out_t is None else out_t + part
    o_ref[...] = take_heads(out_t, heads).T.astype(jnp.bfloat16)


def backward_kernel(
    heads, slots, kb_ref, q_ref, do_ref, kv_ref, p_ref, g_ref, dq_ref, dkv_ref, acc_ref
):
    i = pl.program_id(0)
    width = q_ref.shape[1]

    @pl.when(i == 0)
    def _():
        acc_ref[...] = jnp.zeros_like(acc_ref)

    q_wide = spread_heads(q_ref[...], heads)
    do_wide = spread_heads(do_ref[...], heads)
    pair = 2
    dq_t = None
    for c in range(slots // pair):
        rows = [
            pl.ds(pl.multiple_of(kb_ref[i * slots + c * pair + s] * BLOCK, BLOCK), BLOCK)
            for s in range(pair)
        ]
        keys = jnp.concatenate([kv_ref[r, :width] for r in rows], axis=0)
        vals = jnp.concatenate([kv_ref[r, width:] for r in rows], axis=0)
        at = c * pair * BLOCK
        prob = p_ref[0, at : at + pair * BLOCK, :]
        slope = g_ref[0, at : at + pair * BLOCK, :]
        d_scores = (dot_nt(vals, do_wide) * slope.astype(jnp.float32)).astype(jnp.bfloat16)
        d_vals = jnp.dot(prob, do_wide, preferred_element_type=jnp.float32)
        d_keys = jnp.dot(d_scores, q_wide, preferred_element_type=jnp.float32)
        part = jnp.dot(keys.T, d_scores, preferred_element_type=jnp.float32)
        dq_t = part if dq_t is None else dq_t + part
        for s in range(pair):
            acc_ref[rows[s], :width] += d_keys[s * BLOCK : (s + 1) * BLOCK, :]
            acc_ref[rows[s], width:] += d_vals[s * BLOCK : (s + 1) * BLOCK, :]
    dq_ref[...] = take_heads(dq_t, heads) * SCALING

    @pl.when(i == pl.num_programs(0) - 1)
    def _():
        dkv_ref[:, :width] = (acc_ref[:, :width] * SCALING).astype(jnp.bfloat16)
        dkv_ref[:, width:] = acc_ref[:, width:].astype(jnp.bfloat16)


def attention_forward(key_blocks, weights, query, key_vals, positions_here):
    local_blocks, slots = key_blocks.shape
    width = query.shape[1]
    heads = width // HEAD_DIM
    wide = heads * BLOCK
    whole = pl.BlockSpec(memory_space=pltpu.VMEM)
    smem = pl.BlockSpec(memory_space=pltpu.SMEM)
    stored = jax.ShapeDtypeStruct((local_blocks, slots * BLOCK, wide), jnp.bfloat16)
    return pl.pallas_call(
        functools.partial(forward_kernel, heads, slots),
        grid=(local_blocks,),
        in_specs=[
            smem,
            smem,
            pl.BlockSpec((BLOCK, width), lambda i: (i, 0)),
            whole,
            pl.BlockSpec((BLOCK, 1), lambda i: (i, 0)),
            pl.BlockSpec((1, 1, BLOCK), lambda i: (i, 0, 0)),
        ],
        out_specs=[
            pl.BlockSpec((BLOCK, width), lambda i: (i, 0)),
            pl.BlockSpec((1, slots * BLOCK, wide), lambda i: (i, 0, 0)),
            pl.BlockSpec((1, slots * BLOCK, wide), lambda i: (i, 0, 0)),
        ],
        out_shape=[jax.ShapeDtypeStruct(query.shape, jnp.bfloat16), stored, stored],
        compiler_params=pltpu.CompilerParams(vmem_limit_bytes=48 * 1024 * 1024),
        name="attention_forward",
    )(
        key_blocks.reshape(-1),
        weights.reshape(-1),
        query,
        key_vals,
        positions_here.reshape(-1, 1),
        positions_here.reshape(local_blocks, 1, BLOCK),
    )


def attention_backward(key_blocks, query, d_attended, key_vals, prob, slope):
    local_blocks, slots = key_blocks.shape
    width = query.shape[1]
    heads = width // HEAD_DIM
    wide = heads * BLOCK
    total = key_vals.shape[0]
    whole = pl.BlockSpec(memory_space=pltpu.VMEM)
    smem = pl.BlockSpec(memory_space=pltpu.SMEM)
    block = pl.BlockSpec((BLOCK, width), lambda i: (i, 0))
    stored = pl.BlockSpec((1, slots * BLOCK, wide), lambda i: (i, 0, 0))
    return pl.pallas_call(
        functools.partial(backward_kernel, heads, slots),
        grid=(local_blocks,),
        in_specs=[smem, block, block, whole, stored, stored],
        out_specs=[pl.BlockSpec((width, BLOCK), lambda i: (0, i)), whole],
        out_shape=[
            jax.ShapeDtypeStruct((width, query.shape[0]), jnp.float32),
            jax.ShapeDtypeStruct((total, 2 * width), jnp.bfloat16),
        ],
        scratch_shapes=[pltpu.VMEM((total, 2 * width), jnp.float32)],
        compiler_params=pltpu.CompilerParams(vmem_limit_bytes=48 * 1024 * 1024),
        name="attention_backward",
    )(key_blocks.reshape(-1), query, d_attended, key_vals, prob, slope)


def greet(peers):
    barrier = pltpu.get_barrier_semaphore()
    for peer in peers:
        pl.semaphore_signal(
            barrier, inc=1, device_id=peer, device_id_type=pl.DeviceIdType.MESH
        )
    pl.semaphore_wait(barrier, len(peers))


def send(source, target, send_sem, recv_sem, peer):
    copy = pltpu.make_async_remote_copy(
        src_ref=source,
        dst_ref=target,
        send_sem=send_sem,
        recv_sem=recv_sem,
        device_id=peer,
        device_id_type=pl.DeviceIdType.MESH,
    )
    copy.start()
    return copy


def blk_partners(here):
    return here + 1 - 2 * lax.rem(here, 2), lax.rem(here + 2, 4)


def middle_kernel(
    count,
    att_ref,
    tok_ref,
    gate_ref,
    dg_ref,
    wout_ref,
    mixed_ref,
    grad_u_ref,
    d_heads_ref,
    att_in,
    d_out,
    normed_ref,
    gated_ref,
    local_sem,
    att_sem,
    d_sem,
):
    me = lax.axis_index("head")
    features = att_in.shape[2]
    local_rows = tok_ref.shape[0]
    others = [lax.rem(me + k, count) for k in range(1, count)]
    greet([{"head": other} for other in others])
    local = pltpu.make_async_copy(att_ref.at[me], att_in.at[me], local_sem.at[0])
    local.start()
    copies = [
        send(att_ref.at[other], att_in.at[me], att_sem.at[0, k], att_sem.at[1, k], {"head": other})
        for k, other in enumerate(others)
    ]
    local.wait()
    for copy in copies:
        copy.wait()
    step = 64
    for start in range(0, local_rows, step):
        rows = slice(start, start + step)
        attended = jnp.concatenate([att_in[j, rows, :] for j in range(count)], axis=1)
        attended = attended.astype(jnp.float32)
        average = jnp.mean(attended, axis=1, keepdims=True)
        centered = attended - average
        variance = jnp.mean(centered * centered, axis=1, keepdims=True)
        inverse_std = lax.rsqrt(variance + epsilon)
        normed = centered * inverse_std
        gate = gate_ref[rows, :].astype(jnp.float32)
        normed_ref[rows, :] = normed
        gated_ref[rows, :] = (normed * gate).astype(jnp.bfloat16)
        d_normed = dg_ref[rows, :] * gate
        d_attended = inverse_std * (
            d_normed
            - jnp.mean(d_normed, axis=1, keepdims=True)
            - normed * jnp.mean(d_normed * normed, axis=1, keepdims=True)
        )
        d_attended = d_attended.astype(jnp.bfloat16)
        for j in range(count):
            d_out[j, rows, :] = d_attended[:, j * features : (j + 1) * features]
    local = pltpu.make_async_copy(d_out.at[me], d_heads_ref.at[me], local_sem.at[1])
    local.start()
    copies = [
        send(d_out.at[other], d_heads_ref.at[me], d_sem.at[0, k], d_sem.at[1, k], {"head": other})
        for k, other in enumerate(others)
    ]
    mixed = jnp.dot(gated_ref[...], wout_ref[...], preferred_element_type=jnp.float32)
    mixed_ref[...] = (tok_ref[...].astype(jnp.float32) + mixed).astype(jnp.bfloat16)
    grad_u_ref[...] = (dg_ref[...] * normed_ref[...]).T.astype(jnp.bfloat16)
    local.wait()
    for copy in copies:
        copy.wait()


def middle(attended, tokens, gate_u, d_gated, w_out):
    count = attended.shape[0]
    local_rows, width = tokens.shape
    anywhere = pl.BlockSpec(memory_space=pl.ANY)
    vmem = pl.BlockSpec(memory_space=pltpu.VMEM)
    pair = pltpu.SemaphoreType.DMA((2, count - 1))
    return pl.pallas_call(
        functools.partial(middle_kernel, count),
        in_specs=[anywhere, vmem, vmem, vmem, vmem],
        out_specs=[vmem, vmem, anywhere],
        out_shape=[
            jax.ShapeDtypeStruct(tokens.shape, jnp.bfloat16),
            jax.ShapeDtypeStruct((width, local_rows), jnp.bfloat16),
            jax.ShapeDtypeStruct(attended.shape, jnp.bfloat16),
        ],
        scratch_shapes=[
            pltpu.VMEM(attended.shape, jnp.bfloat16),
            pltpu.VMEM(attended.shape, jnp.bfloat16),
            pltpu.VMEM((local_rows, width), jnp.float32),
            pltpu.VMEM((local_rows, width), jnp.bfloat16),
            pltpu.SemaphoreType.DMA((2,)),
            pair,
            pair,
        ],
        compiler_params=pltpu.CompilerParams(
            collective_id=1, has_side_effects=True, vmem_limit_bytes=48 * 1024 * 1024
        ),
        name="middle",
    )(attended, tokens, gate_u, d_gated, w_out)


def distribute_kernel(
    count,
    features,
    tok_ref,
    w_ref,
    wout_ref,
    cot_ref,
    kv_out,
    q_out,
    gate_ref,
    dg_ref,
    w_buf,
    kv_buf,
    q_buf,
    w_sem,
    local_sem,
    kv_sem,
    q_sem,
    side_sem,
    core_sem,
    pass_sem,
):
    me, here = lax.axis_index("head"), lax.axis_index("blk")
    core, side = blk_partners(here)
    rows, width = tok_ref.shape
    lanes = 128
    per = lanes // features
    groups = count // per
    own_group, own_member = lax.div(me, per), lax.rem(me, per)

    def fetch(first, last, sem):
        columns = pl.ds(first * width, (last - first) * width)
        copy = pltpu.make_async_copy(w_ref.at[:, columns], w_buf.at[:, columns], sem)
        copy.start()
        return copy

    fetches = [fetch(2, 4, w_sem.at[0]), fetch(1, 2, w_sem.at[1]), fetch(0, 1, w_sem.at[2])]
    others = [lax.rem(me + k, count) for k in range(1, count)]
    greet([{"head": other} for other in others] + [{"blk": core}, {"blk": side}])

    def place(segment, source):
        start = pl.multiple_of((segment * count + source) * rows, rows)
        return kv_out.at[pl.ds(start, rows), :]

    def target(k, j):
        group = lax.rem(own_group + k, groups)
        return group * per + lax.rem(own_member + j, per)

    def source(k, j):
        group = lax.rem(own_group - k + groups, groups)
        return group * per + lax.rem(own_member - j + per, per)

    def silu_dot(weights):
        product = jnp.dot(tok_ref[...], weights, preferred_element_type=jnp.float32)
        half = 0.5 * product
        return (half + half * jnp.tanh(half)).astype(jnp.bfloat16)

    def columns_of(part, group):
        start = pl.multiple_of(part * width + group * lanes, lanes)
        return w_buf[:, pl.ds(start, lanes)]

    kv_copies, q_copies = [], []
    fetches[0].wait()
    for k in range(groups):
        group = lax.rem(own_group + k, groups)
        both = silu_dot(jnp.concatenate([columns_of(2, group), columns_of(3, group)], axis=1))
        for j in range(per):
            keys = both[:, j * features : (j + 1) * features]
            vals = both[:, lanes + j * features : lanes + (j + 1) * features]
            kv_buf[group * per + j] = jnp.concatenate([keys, vals], axis=1)
        for j in range(per):
            to, index = target(k, j), k * per + j
            if index == 0:
                local_kv = pltpu.make_async_copy(
                    kv_buf.at[me], place(here, me), local_sem.at[0]
                )
                local_kv.start()
                kv_copies.append(local_kv)
            else:
                kv_copies.append(
                    send(
                        kv_buf.at[to],
                        place(here, me),
                        kv_sem.at[0, index],
                        kv_sem.at[1, index],
                        {"head": to},
                    )
                )
    fetches[1].wait()
    for k in range(groups):
        group = lax.rem(own_group + k, groups)
        query = silu_dot(columns_of(1, group))
        for j in range(per):
            q_buf[group * per + j] = query[:, j * features : (j + 1) * features]
        for j in range(per):
            to, index = target(k, j), k * per + j
            if index == 0:
                local_q = pltpu.make_async_copy(q_buf.at[me], q_out.at[me], local_sem.at[1])
                local_q.start()
            else:
                q_copies.append(
                    send(
                        q_buf.at[to],
                        q_out.at[me],
                        q_sem.at[0, index],
                        q_sem.at[1, index],
                        {"head": to},
                    )
                )
    side_copies, core_copies, pass_copies = [], [], []
    lag = 2
    for index in range(count + lag):
        if index < count:
            if index == 0:
                local_kv.wait()
            else:
                kv_copies[index].wait_recv()
            chunk = place(here, source(index // per, index % per))
            side_copies.append(
                send(chunk, chunk, side_sem.at[0, index], side_sem.at[1, index], {"blk": side})
            )
            core_copies.append(
                send(chunk, chunk, core_sem.at[0, index], core_sem.at[1, index], {"blk": core})
            )
        if index == 1:
            fetches[2].wait()
            for c in range(0, width, 256):
                gate_ref[:, c : c + 256] = silu_dot(w_buf[:, c : c + 256])
        if index == 2:
            for c in range(0, width, 256):
                dg_ref[:, c : c + 256] = dot_nt(cot_ref[...], wout_ref[c : c + 256, :])
        j = index - lag
        if j >= 0:
            side_copies[j].wait_recv()
            chunk = place(side, source(j // per, j % per))
            pass_copies.append(
                send(chunk, chunk, pass_sem.at[0, j], pass_sem.at[1, j], {"blk": core})
            )
    local_q.wait()
    for copy in kv_copies[1:] + side_copies:
        copy.wait_send()
    for copy in q_copies + core_copies + pass_copies:
        copy.wait()


def distribute(tokens, w_proj, w_out, cotangent, count, groups):
    rows, width = tokens.shape
    features = width // count
    anywhere = pl.BlockSpec(memory_space=pl.ANY)
    vmem = pl.BlockSpec(memory_space=pltpu.VMEM)
    pair = pltpu.SemaphoreType.DMA((2, count))
    return pl.pallas_call(
        functools.partial(distribute_kernel, count, features),
        in_specs=[vmem, anywhere, vmem, vmem],
        out_specs=[anywhere, anywhere, vmem, vmem],
        out_shape=[
            jax.ShapeDtypeStruct((groups * count * rows, 2 * features), jnp.bfloat16),
            jax.ShapeDtypeStruct((count, rows, features), jnp.bfloat16),
            jax.ShapeDtypeStruct((rows, width), jnp.bfloat16),
            jax.ShapeDtypeStruct((rows, width), jnp.float32),
        ],
        scratch_shapes=[
            pltpu.VMEM(w_proj.shape, jnp.bfloat16),
            pltpu.VMEM((count, rows, 2 * features), jnp.bfloat16),
            pltpu.VMEM((count, rows, features), jnp.bfloat16),
            pltpu.SemaphoreType.DMA((3,)),
            pltpu.SemaphoreType.DMA((2,)),
            pair,
            pair,
            pair,
            pair,
            pair,
        ],
        compiler_params=pltpu.CompilerParams(
            collective_id=0, has_side_effects=True, vmem_limit_bytes=48 * 1024 * 1024
        ),
        name="distribute",
    )(tokens, w_proj, w_out, cotangent)


def collect_kernel(
    chunks, part_ref, dq_ref, o_ref, core_in, side_out, side_in, near_sem, far_sem, side_sem
):
    here = lax.axis_index("blk")
    core, side = blk_partners(here)
    far = lax.rem(core + 2, 4)
    width, segment = dq_ref.shape
    rows = segment // chunks
    greet([{"blk": core}, {"blk": side}])
    far_copies = [
        send(
            part_ref.at[far, c], core_in.at[1, c], far_sem.at[0, c], far_sem.at[1, c], {"blk": core}
        )
        for c in range(chunks)
    ]
    near_copies = [
        send(
            part_ref.at[core, c],
            core_in.at[0, c],
            near_sem.at[0, c],
            near_sem.at[1, c],
            {"blk": core},
        )
        for c in range(chunks)
    ]
    side_copies = []
    for c in range(chunks):
        far_copies[c].wait_recv()
        total = part_ref[side, c].astype(jnp.float32) + core_in[1, c].astype(jnp.float32)
        side_out[c] = total.astype(jnp.bfloat16)
        side_copies.append(
            send(
                side_out.at[c], side_in.at[c], side_sem.at[0, c], side_sem.at[1, c], {"blk": side}
            )
        )
    o_ref[:width, :] = dq_ref[...]
    for c in range(chunks):
        near_copies[c].wait_recv()
        side_copies[c].wait_recv()
        total = (
            part_ref[here, c].astype(jnp.float32)
            + core_in[0, c].astype(jnp.float32)
            + side_in[c].astype(jnp.float32)
        )
        o_ref[width:, c * rows : (c + 1) * rows] = total.T
    for copy in far_copies + near_copies + side_copies:
        copy.wait_send()


def collect(partial, grad_query, groups):
    width, segment = grad_query.shape
    chunks = 8
    rows = segment // chunks
    vmem = pl.BlockSpec(memory_space=pltpu.VMEM)
    pair = pltpu.SemaphoreType.DMA((2, chunks))
    block = (chunks, rows, 2 * width)
    return pl.pallas_call(
        functools.partial(collect_kernel, chunks),
        in_specs=[vmem, vmem],
        out_specs=vmem,
        out_shape=jax.ShapeDtypeStruct((3 * width, segment), jnp.float32),
        scratch_shapes=[
            pltpu.VMEM((2,) + block, jnp.bfloat16),
            pltpu.VMEM(block, jnp.bfloat16),
            pltpu.VMEM(block, jnp.bfloat16),
            pair,
            pair,
            pair,
        ],
        compiler_params=pltpu.CompilerParams(
            collective_id=2, has_side_effects=True, vmem_limit_bytes=48 * 1024 * 1024
        ),
        name="collect",
    )(partial.reshape((groups,) + block), grad_query)


def shards(tokens, w_proj, w_out, cotangent, key_blocks, exposures, positions):
    head_count = lax.axis_size("head")
    group_count = lax.axis_size("blk")
    segment_index = lax.axis_index("blk")
    local_rows, width = tokens.shape
    features = width // head_count
    segment = local_rows * head_count
    key_all, query, gate_u, d_gated = distribute(
        tokens, w_proj, w_out, cotangent, head_count, group_count
    )
    query = query.reshape(segment, features)
    positions_here = lax.dynamic_slice_in_dim(positions, segment_index * segment, segment, 0)
    weights = jnp.log1p(exposures.astype(jnp.float32))
    attended, prob, slope = attention_forward(
        key_blocks, weights, query, key_all, positions_here
    )
    mixed, grad_u, d_heads = middle(
        attended.reshape(head_count, local_rows, features), tokens, gate_u, d_gated, w_out
    )
    d_heads = d_heads.reshape(segment, features)
    grad_query, partial = attention_backward(
        key_blocks, query, d_heads, key_all, prob, slope
    )
    grad_qkv = collect(partial, grad_query, group_count).reshape(3, features, segment)
    return (mixed, grad_u, grad_qkv)


def solution(mesh):
    in_specs = (
        P(("blk", "head"), None),
        P(),
        P(),
        P(("blk", "head"), None),
        P("blk", None),
        P("blk", None),
        P(),
    )
    out_specs = (P(("blk", "head"), None), P(None, ("blk", "head")), P(None, "head", "blk"))
    return jax.shard_map(shards, mesh=mesh, in_specs=in_specs, out_specs=out_specs, check_vma=False)
```

```python
import functools

import jax
import jax.numpy as jnp
from jax import lax
from jax.experimental import pallas as pl
from jax.experimental.pallas import tpu as pltpu
from jax.sharding import PartitionSpec as P

HEADS = 32
HEAD_DIM = 32
BLOCK = 128
SCALING = HEAD_DIM ** (-0.5)
epsilon = 1e-05


def dot_nt(a, b):
    return lax.dot_general(a, b, (((1,), (1,)), ((), ())), preferred_element_type=jnp.float32)


def spread_heads(block, heads):
    head_of = lax.broadcasted_iota(jnp.int32, block.shape, 1) // HEAD_DIM
    return jnp.concatenate(
        [jnp.where(head_of == h, block, jnp.zeros_like(block)) for h in range(heads)], axis=0
    )


def take_heads(wide, heads):
    return jnp.concatenate(
        [
            wide[h * HEAD_DIM : (h + 1) * HEAD_DIM, h * BLOCK : (h + 1) * BLOCK]
            for h in range(heads)
        ],
        axis=0,
    )


def forward_block(heads, slots, i, kb_ref, wt_ref, query, kv_ref, posc, posr, p_ref, g_ref):
    width = query.shape[1]
    q_wide = spread_heads(query, heads)
    pair = 2
    out_t = None
    for c in range(slots // pair):
        tables = [kv_ref[kb_ref[i * slots + c * pair + s]] for s in range(pair)]
        keys = jnp.concatenate([table[:, :width] for table in tables], axis=0)
        vals = jnp.concatenate([table[:, width:] for table in tables], axis=0)
        scores = dot_nt(keys, q_wide)
        probs = []
        for s in range(pair):
            weight = wt_ref[i * slots + c * pair + s]
            half = scores[s * BLOCK : (s + 1) * BLOCK, :] * (0.5 * SCALING)
            up = 1.0 + jnp.tanh(half)
            hu = half * up
            slope = up + hu * (2.0 - up)
            if c == 0 and s == 0:
                coefficient = jnp.where(posc <= posr, weight, 0.0)
                coefficient = jnp.concatenate([coefficient] * heads, axis=1)
            else:
                coefficient = weight
            prob = (hu * coefficient).astype(jnp.bfloat16)
            at = (c * pair + s) * BLOCK
            p_ref[at : at + BLOCK, :] = prob
            g_ref[at : at + BLOCK, :] = (slope * (0.5 * coefficient)).astype(jnp.bfloat16)
            probs.append(prob)
        part = jnp.dot(vals.T, jnp.concatenate(probs, axis=0), preferred_element_type=jnp.float32)
        out_t = part if out_t is None else out_t + part
    return take_heads(out_t, heads).T.astype(jnp.bfloat16)


def backward_kernel(
    heads, slots, kb_ref, q_ref, do_ref, kv_ref, p_ref, g_ref, dq_ref, dkv_ref, acc_ref
):
    i = pl.program_id(0)
    width = q_ref.shape[1]

    @pl.when(i == 0)
    def _():
        acc_ref[...] = jnp.zeros_like(acc_ref)

    q_wide = spread_heads(q_ref[...], heads)
    do_wide = spread_heads(do_ref[...], heads)
    pair = 2
    dq_t = None
    for c in range(slots // pair):
        rows = [
            pl.ds(pl.multiple_of(kb_ref[i * slots + c * pair + s] * BLOCK, BLOCK), BLOCK)
            for s in range(pair)
        ]
        keys = jnp.concatenate([kv_ref[r, :width] for r in rows], axis=0)
        vals = jnp.concatenate([kv_ref[r, width:] for r in rows], axis=0)
        at = c * pair * BLOCK
        prob = p_ref[0, at : at + pair * BLOCK, :]
        slope = g_ref[0, at : at + pair * BLOCK, :]
        d_scores = (dot_nt(vals, do_wide) * slope.astype(jnp.float32)).astype(jnp.bfloat16)
        d_vals = jnp.dot(prob, do_wide, preferred_element_type=jnp.float32)
        d_keys = jnp.dot(d_scores, q_wide, preferred_element_type=jnp.float32)
        part = jnp.dot(keys.T, d_scores, preferred_element_type=jnp.float32)
        dq_t = part if dq_t is None else dq_t + part
        for s in range(pair):
            acc_ref[rows[s], :width] += d_keys[s * BLOCK : (s + 1) * BLOCK, :]
            acc_ref[rows[s], width:] += d_vals[s * BLOCK : (s + 1) * BLOCK, :]
    dq_ref[...] = take_heads(dq_t, heads) * SCALING

    @pl.when(i == pl.num_programs(0) - 1)
    def _():
        dkv_ref[:, :width] = (acc_ref[:, :width] * SCALING).astype(jnp.bfloat16)
        dkv_ref[:, width:] = acc_ref[:, width:].astype(jnp.bfloat16)


def attention_backward(key_blocks, query, d_attended, key_vals, prob, slope):
    local_blocks, slots = key_blocks.shape
    width = query.shape[1]
    heads = width // HEAD_DIM
    wide = heads * BLOCK
    total = key_vals.shape[0]
    whole = pl.BlockSpec(memory_space=pltpu.VMEM)
    smem = pl.BlockSpec(memory_space=pltpu.SMEM)
    block = pl.BlockSpec((BLOCK, width), lambda i: (i, 0))
    stored = pl.BlockSpec((1, slots * BLOCK, wide), lambda i: (i, 0, 0))
    return pl.pallas_call(
        functools.partial(backward_kernel, heads, slots),
        grid=(local_blocks,),
        in_specs=[smem, block, block, whole, stored, stored],
        out_specs=[pl.BlockSpec((width, BLOCK), lambda i: (0, i)), whole],
        out_shape=[
            jax.ShapeDtypeStruct((width, query.shape[0]), jnp.float32),
            jax.ShapeDtypeStruct((total, 2 * width), jnp.bfloat16),
        ],
        scratch_shapes=[pltpu.VMEM((total, 2 * width), jnp.float32)],
        compiler_params=pltpu.CompilerParams(vmem_limit_bytes=48 * 1024 * 1024),
        name="attention_backward",
    )(key_blocks.reshape(-1), query, d_attended, key_vals, prob, slope)


def greet(peers):
    barrier = pltpu.get_barrier_semaphore()
    for peer in peers:
        pl.semaphore_signal(
            barrier, inc=1, device_id=peer, device_id_type=pl.DeviceIdType.MESH
        )
    pl.semaphore_wait(barrier, len(peers))


def send(source, target, send_sem, recv_sem, peer):
    copy = pltpu.make_async_remote_copy(
        src_ref=source,
        dst_ref=target,
        send_sem=send_sem,
        recv_sem=recv_sem,
        device_id=peer,
        device_id_type=pl.DeviceIdType.MESH,
    )
    copy.start()
    return copy


def blk_partners(here):
    return here + 1 - 2 * lax.rem(here, 2), lax.rem(here + 2, 4)


def middle_kernel(
    count,
    heads,
    slots,
    kb_ref,
    wt_ref,
    q_ref,
    kv_ref,
    posc_ref,
    posr_ref,
    tok_ref,
    gate_ref,
    dg_ref,
    wout_ref,
    mixed_ref,
    grad_u_ref,
    d_heads_ref,
    prob_ref,
    slope_ref,
    p_buf,
    g_buf,
    att_out,
    att_in,
    d_out,
    normed_ref,
    gated_ref,
    local_sem,
    store_sem,
    att_sem,
    d_sem,
):
    me = lax.axis_index("head")
    features = att_in.shape[2]
    local_rows = tok_ref.shape[0]
    per_owner = local_rows // BLOCK
    others = [lax.rem(me + k, count) for k in range(1, count)]
    greet([{"head": other} for other in others])

    def attended_copy(k):
        owner = lax.rem(me + 1 + k, count)
        return pltpu.make_async_remote_copy(
            src_ref=att_out.at[owner],
            dst_ref=att_in.at[me],
            send_sem=att_sem.at[0, k],
            recv_sem=att_sem.at[1, k],
            device_id={"head": owner},
            device_id_type=pl.DeviceIdType.MESH,
        )

    def stores(slot, block):
        return [
            pltpu.make_async_copy(p_buf.at[slot], prob_ref.at[block], store_sem.at[0, slot]),
            pltpu.make_async_copy(g_buf.at[slot], slope_ref.at[block], store_sem.at[1, slot]),
        ]

    def step(t, carry):
        k, r = lax.div(t, per_owner), lax.rem(t, per_owner)
        owner = lax.rem(me + 1 + k, count)
        block = owner * per_owner + r
        slot = lax.rem(t, 2)

        @pl.when(t >= 2)
        def _():
            for copy in stores(slot, block):
                copy.wait()

        rows = pl.ds(pl.multiple_of(block * BLOCK, BLOCK), BLOCK)
        attended = forward_block(
            heads,
            slots,
            block,
            kb_ref,
            wt_ref,
            q_ref[rows, :],
            kv_ref,
            posc_ref[rows, :],
            posr_ref[block],
            p_buf.at[slot],
            g_buf.at[slot],
        )
        att_out[owner, pl.ds(pl.multiple_of(r * BLOCK, BLOCK), BLOCK), :] = attended
        for copy in stores(slot, block):
            copy.start()

        @pl.when((r == per_owner - 1) & (k < count - 1))
        def _():
            attended_copy(k).start()

        return carry

    lax.fori_loop(0, count * per_owner, step, 0)
    att_in[me] = att_out[me]
    for k in range(count - 1):
        attended_copy(k).wait()
    d_copies = []
    step_rows = 64
    half_rows = local_rows // 2
    for part in range(2):
        for start in range(part * half_rows, (part + 1) * half_rows, step_rows):
            rows = slice(start, start + step_rows)
            attended = jnp.concatenate([att_in[j, rows, :] for j in range(count)], axis=1)
            attended = attended.astype(jnp.float32)
            average = jnp.mean(attended, axis=1, keepdims=True)
            centered = attended - average
            variance = jnp.mean(centered * centered, axis=1, keepdims=True)
            inverse_std = lax.rsqrt(variance + epsilon)
            normed = centered * inverse_std
            gate = gate_ref[rows, :].astype(jnp.float32)
            normed_ref[rows, :] = normed
            gated_ref[rows, :] = (normed * gate).astype(jnp.bfloat16)
            d_normed = dg_ref[rows, :] * gate
            d_attended = inverse_std * (
                d_normed
                - jnp.mean(d_normed, axis=1, keepdims=True)
                - normed * jnp.mean(d_normed * normed, axis=1, keepdims=True)
            )
            d_attended = d_attended.astype(jnp.bfloat16)
            for j in range(count):
                d_out[j, rows, :] = d_attended[:, j * features : (j + 1) * features]
        rows = pl.ds(part * half_rows, half_rows)
        local = pltpu.make_async_copy(
            d_out.at[me, rows], d_heads_ref.at[me, rows], local_sem.at[part]
        )
        local.start()
        d_copies.append(local)
        for k, other in enumerate(others):
            d_copies.append(
                send(
                    d_out.at[other, rows],
                    d_heads_ref.at[me, rows],
                    d_sem.at[0, part, k],
                    d_sem.at[1, part, k],
                    {"head": other},
                )
            )
    mixed = jnp.dot(gated_ref[...], wout_ref[...], preferred_element_type=jnp.float32)
    mixed_ref[...] = (tok_ref[...].astype(jnp.float32) + mixed).astype(jnp.bfloat16)
    grad_u_ref[...] = (dg_ref[...] * normed_ref[...]).T.astype(jnp.bfloat16)
    for slot in range(2):
        for copy in stores(slot, me):
            copy.wait()
    for copy in d_copies:
        copy.wait()


def middle(key_blocks, weights, query, key_vals, positions_here, tokens, gate_u, d_gated, w_out):
    local_blocks, slots = key_blocks.shape
    local_rows, width = tokens.shape
    segment, features = query.shape
    heads = features // HEAD_DIM
    count = segment // local_rows
    exchanged = (count, local_rows, features)
    tall, wide = slots * BLOCK, heads * BLOCK
    anywhere = pl.BlockSpec(memory_space=pl.ANY)
    vmem = pl.BlockSpec(memory_space=pltpu.VMEM)
    smem = pl.BlockSpec(memory_space=pltpu.SMEM)
    stored = jax.ShapeDtypeStruct((local_blocks, tall, wide), jnp.bfloat16)
    return pl.pallas_call(
        functools.partial(middle_kernel, count, heads, slots),
        in_specs=[smem, smem] + [vmem] * 8,
        out_specs=[vmem, vmem, anywhere, anywhere, anywhere],
        out_shape=[
            jax.ShapeDtypeStruct(tokens.shape, jnp.bfloat16),
            jax.ShapeDtypeStruct((width, local_rows), jnp.bfloat16),
            jax.ShapeDtypeStruct(exchanged, jnp.bfloat16),
            stored,
            stored,
        ],
        scratch_shapes=[
            pltpu.VMEM((2, tall, wide), jnp.bfloat16),
            pltpu.VMEM((2, tall, wide), jnp.bfloat16),
            pltpu.VMEM(exchanged, jnp.bfloat16),
            pltpu.VMEM(exchanged, jnp.bfloat16),
            pltpu.VMEM(exchanged, jnp.bfloat16),
            pltpu.VMEM((local_rows, width), jnp.float32),
            pltpu.VMEM((local_rows, width), jnp.bfloat16),
            pltpu.SemaphoreType.DMA((2,)),
            pltpu.SemaphoreType.DMA((2, 2)),
            pltpu.SemaphoreType.DMA((2, count - 1)),
            pltpu.SemaphoreType.DMA((2, 2, count - 1)),
        ],
        compiler_params=pltpu.CompilerParams(
            collective_id=1, has_side_effects=True, vmem_limit_bytes=48 * 1024 * 1024
        ),
        name="middle",
    )(
        key_blocks.reshape(-1),
        weights.reshape(-1),
        query,
        key_vals.reshape(-1, BLOCK, 2 * features),
        positions_here.reshape(-1, 1),
        positions_here.reshape(local_blocks, 1, BLOCK),
        tokens,
        gate_u,
        d_gated,
        w_out,
    )


def distribute_kernel(
    count,
    features,
    tok_ref,
    w_ref,
    wout_ref,
    cot_ref,
    kv_out,
    q_out,
    gate_ref,
    dg_ref,
    w_buf,
    wout_buf,
    cot_buf,
    kv_buf,
    q_buf,
    w_sem,
    local_sem,
    kv_sem,
    q_sem,
    side_sem,
    core_sem,
    pass_sem,
):
    me, here = lax.axis_index("head"), lax.axis_index("blk")
    core, side = blk_partners(here)
    rows, width = tok_ref.shape
    lanes = 128
    per = lanes // features
    groups = count // per
    own_group, own_member = lax.div(me, per), lax.rem(me, per)

    def fetch(first, last, sem):
        columns = pl.ds(first * width, (last - first) * width)
        copy = pltpu.make_async_copy(w_ref.at[:, columns], w_buf.at[:, columns], sem)
        copy.start()
        return copy

    fetches = [fetch(2, 4, w_sem.at[0]), fetch(1, 2, w_sem.at[1]), fetch(0, 1, w_sem.at[2])]
    late = [
        pltpu.make_async_copy(wout_ref, wout_buf, w_sem.at[3]),
        pltpu.make_async_copy(cot_ref, cot_buf, w_sem.at[4]),
    ]
    for copy in late:
        copy.start()
    others = [lax.rem(me + k, count) for k in range(1, count)]
    greet([{"head": other} for other in others] + [{"blk": core}, {"blk": side}])

    def place(segment, source):
        start = pl.multiple_of((segment * count + source) * rows, rows)
        return kv_out.at[pl.ds(start, rows), :]

    def target(k, j):
        group = lax.rem(own_group + k, groups)
        return group * per + lax.rem(own_member + j, per)

    def source(k, j):
        group = lax.rem(own_group - k + groups, groups)
        return group * per + lax.rem(own_member - j + per, per)

    def silu_dot(weights):
        product = jnp.dot(tok_ref[...], weights, preferred_element_type=jnp.float32)
        half = 0.5 * product
        return (half + half * jnp.tanh(half)).astype(jnp.bfloat16)

    def columns_of(part, group):
        start = pl.multiple_of(part * width + group * lanes, lanes)
        return w_buf[:, pl.ds(start, lanes)]

    kv_copies, q_copies = [], []
    fetches[0].wait()
    for k in range(groups):
        group = lax.rem(own_group + k, groups)
        both = silu_dot(jnp.concatenate([columns_of(2, group), columns_of(3, group)], axis=1))
        for j in range(per):
            keys = both[:, j * features : (j + 1) * features]
            vals = both[:, lanes + j * features : lanes + (j + 1) * features]
            kv_buf[group * per + j] = jnp.concatenate([keys, vals], axis=1)
        for j in range(per):
            to, index = target(k, j), k * per + j
            if index == 0:
                local_kv = pltpu.make_async_copy(
                    kv_buf.at[me], place(here, me), local_sem.at[0]
                )
                local_kv.start()
                kv_copies.append(local_kv)
            else:
                kv_copies.append(
                    send(
                        kv_buf.at[to],
                        place(here, me),
                        kv_sem.at[0, index],
                        kv_sem.at[1, index],
                        {"head": to},
                    )
                )
    fetches[1].wait()
    for k in range(groups):
        group = lax.rem(own_group + k, groups)
        query = silu_dot(columns_of(1, group))
        for j in range(per):
            q_buf[group * per + j] = query[:, j * features : (j + 1) * features]
        for j in range(per):
            to, index = target(k, j), k * per + j
            if index == 0:
                local_q = pltpu.make_async_copy(q_buf.at[me], q_out.at[me], local_sem.at[1])
                local_q.start()
            else:
                q_copies.append(
                    send(
                        q_buf.at[to],
                        q_out.at[me],
                        q_sem.at[0, index],
                        q_sem.at[1, index],
                        {"head": to},
                    )
                )
    side_copies, core_copies, pass_copies = [], [], []
    lag = 2
    for index in range(count + lag):
        if index < count:
            if index == 0:
                local_kv.wait()
            else:
                kv_copies[index].wait_recv()
            chunk = place(here, source(index // per, index % per))
            side_copies.append(
                send(chunk, chunk, side_sem.at[0, index], side_sem.at[1, index], {"blk": side})
            )
            core_copies.append(
                send(chunk, chunk, core_sem.at[0, index], core_sem.at[1, index], {"blk": core})
            )
        if index == 1:
            fetches[2].wait()
            for c in range(0, width, 256):
                gate_ref[:, c : c + 256] = silu_dot(w_buf[:, c : c + 256])
        if index == 2:
            for copy in late:
                copy.wait()
            for c in range(0, width, 256):
                dg_ref[:, c : c + 256] = dot_nt(cot_buf[...], wout_buf[c : c + 256, :])
        j = index - lag
        if j >= 0:
            side_copies[j].wait_recv()
            chunk = place(side, source(j // per, j % per))
            pass_copies.append(
                send(chunk, chunk, pass_sem.at[0, j], pass_sem.at[1, j], {"blk": core})
            )
    local_q.wait()
    for copy in kv_copies[1:] + side_copies:
        copy.wait_send()
    for copy in q_copies + core_copies + pass_copies:
        copy.wait()


def distribute(tokens, w_proj, w_out, cotangent, count, groups):
    rows, width = tokens.shape
    features = width // count
    anywhere = pl.BlockSpec(memory_space=pl.ANY)
    vmem = pl.BlockSpec(memory_space=pltpu.VMEM)
    pair = pltpu.SemaphoreType.DMA((2, count))
    return pl.pallas_call(
        functools.partial(distribute_kernel, count, features),
        in_specs=[vmem, anywhere, anywhere, anywhere],
        out_specs=[anywhere, anywhere, vmem, vmem],
        out_shape=[
            jax.ShapeDtypeStruct((groups * count * rows, 2 * features), jnp.bfloat16),
            jax.ShapeDtypeStruct((count, rows, features), jnp.bfloat16),
            jax.ShapeDtypeStruct((rows, width), jnp.bfloat16),
            jax.ShapeDtypeStruct((rows, width), jnp.float32),
        ],
        scratch_shapes=[
            pltpu.VMEM(w_proj.shape, jnp.bfloat16),
            pltpu.VMEM(w_out.shape, jnp.bfloat16),
            pltpu.VMEM(cotangent.shape, jnp.bfloat16),
            pltpu.VMEM((count, rows, 2 * features), jnp.bfloat16),
            pltpu.VMEM((count, rows, features), jnp.bfloat16),
            pltpu.SemaphoreType.DMA((5,)),
            pltpu.SemaphoreType.DMA((2,)),
            pair,
            pair,
            pair,
            pair,
            pair,
        ],
        compiler_params=pltpu.CompilerParams(
            collective_id=0, has_side_effects=True, vmem_limit_bytes=48 * 1024 * 1024
        ),
        name="distribute",
    )(tokens, w_proj, w_out, cotangent)


def collect_kernel(
    chunks, part_ref, dq_ref, o_ref, core_in, side_out, side_in, near_sem, far_sem, side_sem
):
    here = lax.axis_index("blk")
    core, side = blk_partners(here)
    far = lax.rem(core + 2, 4)
    width, segment = dq_ref.shape
    rows = segment // chunks
    greet([{"blk": core}, {"blk": side}])
    far_copies = [
        send(
            part_ref.at[far, c], core_in.at[1, c], far_sem.at[0, c], far_sem.at[1, c], {"blk": core}
        )
        for c in range(chunks)
    ]
    near_copies = [
        send(
            part_ref.at[core, c],
            core_in.at[0, c],
            near_sem.at[0, c],
            near_sem.at[1, c],
            {"blk": core},
        )
        for c in range(chunks)
    ]
    side_copies = []
    for c in range(chunks):
        far_copies[c].wait_recv()
        total = part_ref[side, c].astype(jnp.float32) + core_in[1, c].astype(jnp.float32)
        side_out[c] = total.astype(jnp.bfloat16)
        side_copies.append(
            send(
                side_out.at[c], side_in.at[c], side_sem.at[0, c], side_sem.at[1, c], {"blk": side}
            )
        )
    o_ref[:width, :] = dq_ref[...]
    for c in range(chunks):
        near_copies[c].wait_recv()
        side_copies[c].wait_recv()
        total = (
            part_ref[here, c].astype(jnp.float32)
            + core_in[0, c].astype(jnp.float32)
            + side_in[c].astype(jnp.float32)
        )
        o_ref[width:, c * rows : (c + 1) * rows] = total.T
    for copy in far_copies + near_copies + side_copies:
        copy.wait_send()


def collect(partial, grad_query, groups):
    width, segment = grad_query.shape
    chunks = 8
    rows = segment // chunks
    vmem = pl.BlockSpec(memory_space=pltpu.VMEM)
    pair = pltpu.SemaphoreType.DMA((2, chunks))
    block = (chunks, rows, 2 * width)
    return pl.pallas_call(
        functools.partial(collect_kernel, chunks),
        in_specs=[vmem, vmem],
        out_specs=vmem,
        out_shape=jax.ShapeDtypeStruct((3 * width, segment), jnp.float32),
        scratch_shapes=[
            pltpu.VMEM((2,) + block, jnp.bfloat16),
            pltpu.VMEM(block, jnp.bfloat16),
            pltpu.VMEM(block, jnp.bfloat16),
            pair,
            pair,
            pair,
        ],
        compiler_params=pltpu.CompilerParams(
            collective_id=2, has_side_effects=True, vmem_limit_bytes=48 * 1024 * 1024
        ),
        name="collect",
    )(partial.reshape((groups,) + block), grad_query)


def shards(tokens, w_proj, w_out, cotangent, key_blocks, exposures, positions):
    head_count = lax.axis_size("head")
    group_count = lax.axis_size("blk")
    segment_index = lax.axis_index("blk")
    local_rows, width = tokens.shape
    features = width // head_count
    segment = local_rows * head_count
    key_all, query, gate_u, d_gated = distribute(
        tokens, w_proj, w_out, cotangent, head_count, group_count
    )
    query = query.reshape(segment, features)
    positions_here = lax.dynamic_slice_in_dim(positions, segment_index * segment, segment, 0)
    weights = jnp.log1p(exposures.astype(jnp.float32))
    mixed, grad_u, d_heads, prob, slope = middle(
        key_blocks, weights, query, key_all, positions_here, tokens, gate_u, d_gated, w_out
    )
    d_heads = d_heads.reshape(segment, features)
    grad_query, partial = attention_backward(
        key_blocks, query, d_heads, key_all, prob, slope
    )
    grad_qkv = collect(partial, grad_query, group_count).reshape(3, features, segment)
    return (mixed, grad_u, grad_qkv)


def solution(mesh):
    in_specs = (
        P(("blk", "head"), None),
        P(),
        P(),
        P(("blk", "head"), None),
        P("blk", None),
        P("blk", None),
        P(),
    )
    out_specs = (P(("blk", "head"), None), P(None, ("blk", "head")), P(None, "head", "blk"))
    return jax.shard_map(shards, mesh=mesh, in_specs=in_specs, out_specs=out_specs, check_vma=False)
```

```python
import functools

import jax
import jax.numpy as jnp
from jax import lax
from jax.experimental import pallas as pl
from jax.experimental.pallas import tpu as pltpu
from jax.sharding import PartitionSpec as P

HEADS = 32
HEAD_DIM = 32
BLOCK = 128
SCALING = HEAD_DIM ** (-0.5)
epsilon = 1e-05


def dot_nt(a, b):
    return lax.dot_general(a, b, (((1,), (1,)), ((), ())), preferred_element_type=jnp.float32)


def spread_heads(block, heads):
    head_of = lax.broadcasted_iota(jnp.int32, block.shape, 1) // HEAD_DIM
    return jnp.concatenate(
        [jnp.where(head_of == h, block, jnp.zeros_like(block)) for h in range(heads)], axis=0
    )


def take_heads(wide, heads):
    return jnp.concatenate(
        [
            wide[h * HEAD_DIM : (h + 1) * HEAD_DIM, h * BLOCK : (h + 1) * BLOCK]
            for h in range(heads)
        ],
        axis=0,
    )


def forward_block(heads, slots, i, kb_ref, wt_ref, query, kv_ref, posc, posr, p_ref, g_ref):
    width = query.shape[1]
    q_wide = spread_heads(query, heads)
    pair = 2
    out_t = None

    def pair_scores(c):
        tables = [kv_ref[kb_ref[i * slots + c * pair + s]] for s in range(pair)]
        keys = jnp.concatenate([table[:, :width] for table in tables], axis=0)
        vals = jnp.concatenate([table[:, width:] for table in tables], axis=0)
        return dot_nt(keys, q_wide), vals

    ahead = pair_scores(0)
    for c in range(slots // pair):
        scores, vals = ahead
        if c + 1 < slots // pair:
            ahead = pair_scores(c + 1)
        probs = []
        for s in range(pair):
            weight = wt_ref[i * slots + c * pair + s]
            half = scores[s * BLOCK : (s + 1) * BLOCK, :] * (0.5 * SCALING)
            up = 1.0 + jnp.tanh(half)
            hu = half * up
            slope = up + hu * (2.0 - up)
            if c == 0 and s == 0:
                coefficient = jnp.where(posc <= posr, weight, 0.0)
                coefficient = jnp.concatenate([coefficient] * heads, axis=1)
            else:
                coefficient = weight
            prob = (hu * coefficient).astype(jnp.bfloat16)
            at = (c * pair + s) * BLOCK
            p_ref[at : at + BLOCK, :] = prob
            g_ref[at : at + BLOCK, :] = (slope * (0.5 * coefficient)).astype(jnp.bfloat16)
            probs.append(prob)
        part = jnp.dot(vals.T, jnp.concatenate(probs, axis=0), preferred_element_type=jnp.float32)
        out_t = part if out_t is None else out_t + part
    return take_heads(out_t, heads).T.astype(jnp.bfloat16)


def backward_kernel(
    heads, slots, kb_ref, q_ref, do_ref, kv_ref, p_ref, g_ref, dq_ref, dkv_ref, acc_ref
):
    i = pl.program_id(0)
    width = q_ref.shape[1]

    @pl.when(i == 0)
    def _():
        acc_ref[...] = jnp.zeros_like(acc_ref)

    q_wide = spread_heads(q_ref[...], heads)
    do_wide = spread_heads(do_ref[...], heads)
    pair = 2
    dq_t = None

    def pair_d_probs(c):
        rows = [
            pl.ds(pl.multiple_of(kb_ref[i * slots + c * pair + s] * BLOCK, BLOCK), BLOCK)
            for s in range(pair)
        ]
        keys = jnp.concatenate([kv_ref[r, :width] for r in rows], axis=0)
        vals = jnp.concatenate([kv_ref[r, width:] for r in rows], axis=0)
        return rows, keys, dot_nt(vals, do_wide)

    ahead = pair_d_probs(0)
    for c in range(slots // pair):
        rows, keys, d_probs = ahead
        if c + 1 < slots // pair:
            ahead = pair_d_probs(c + 1)
        at = c * pair * BLOCK
        prob = p_ref[0, at : at + pair * BLOCK, :]
        slope = g_ref[0, at : at + pair * BLOCK, :]
        d_scores = (d_probs * slope.astype(jnp.float32)).astype(jnp.bfloat16)
        d_vals = jnp.dot(prob, do_wide, preferred_element_type=jnp.float32)
        d_keys = jnp.dot(d_scores, q_wide, preferred_element_type=jnp.float32)
        part = jnp.dot(keys.T, d_scores, preferred_element_type=jnp.float32)
        dq_t = part if dq_t is None else dq_t + part
        for s in range(pair):
            acc_ref[rows[s], :width] += d_keys[s * BLOCK : (s + 1) * BLOCK, :]
            acc_ref[rows[s], width:] += d_vals[s * BLOCK : (s + 1) * BLOCK, :]
    dq_ref[...] = take_heads(dq_t, heads) * SCALING

    @pl.when(i == pl.num_programs(0) - 1)
    def _():
        dkv_ref[:, :width] = (acc_ref[:, :width] * SCALING).astype(jnp.bfloat16)
        dkv_ref[:, width:] = acc_ref[:, width:].astype(jnp.bfloat16)


def attention_backward(key_blocks, query, d_attended, key_vals, prob, slope):
    local_blocks, slots = key_blocks.shape
    width = query.shape[1]
    heads = width // HEAD_DIM
    wide = heads * BLOCK
    total = key_vals.shape[0]
    whole = pl.BlockSpec(memory_space=pltpu.VMEM)
    smem = pl.BlockSpec(memory_space=pltpu.SMEM)
    block = pl.BlockSpec((BLOCK, width), lambda i: (i, 0))
    stored = pl.BlockSpec((1, slots * BLOCK, wide), lambda i: (i, 0, 0))
    return pl.pallas_call(
        functools.partial(backward_kernel, heads, slots),
        grid=(local_blocks,),
        in_specs=[smem, block, block, whole, stored, stored],
        out_specs=[pl.BlockSpec((width, BLOCK), lambda i: (0, i)), whole],
        out_shape=[
            jax.ShapeDtypeStruct((width, query.shape[0]), jnp.float32),
            jax.ShapeDtypeStruct((total, 2 * width), jnp.bfloat16),
        ],
        scratch_shapes=[pltpu.VMEM((total, 2 * width), jnp.float32)],
        compiler_params=pltpu.CompilerParams(vmem_limit_bytes=48 * 1024 * 1024),
        name="attention_backward",
    )(key_blocks.reshape(-1), query, d_attended, key_vals, prob, slope)


def greet(peers):
    barrier = pltpu.get_barrier_semaphore()
    for peer in peers:
        pl.semaphore_signal(
            barrier, inc=1, device_id=peer, device_id_type=pl.DeviceIdType.MESH
        )
    pl.semaphore_wait(barrier, len(peers))


def send(source, target, send_sem, recv_sem, peer):
    copy = pltpu.make_async_remote_copy(
        src_ref=source,
        dst_ref=target,
        send_sem=send_sem,
        recv_sem=recv_sem,
        device_id=peer,
        device_id_type=pl.DeviceIdType.MESH,
    )
    copy.start()
    return copy


def blk_partners(here):
    return here + 1 - 2 * lax.rem(here, 2), lax.rem(here + 2, 4)


def middle_kernel(
    count,
    heads,
    slots,
    kb_ref,
    wt_ref,
    q_ref,
    kv_ref,
    posc_ref,
    posr_ref,
    tok_ref,
    gate_ref,
    dg_ref,
    wout_ref,
    mixed_ref,
    grad_u_ref,
    d_heads_ref,
    prob_ref,
    slope_ref,
    p_buf,
    g_buf,
    att_out,
    att_in,
    d_out,
    normed_ref,
    gated_ref,
    local_sem,
    store_sem,
    att_sem,
    d_sem,
):
    me = lax.axis_index("head")
    features = att_in.shape[2]
    local_rows = tok_ref.shape[0]
    per_owner = local_rows // BLOCK
    others = [lax.rem(me + k, count) for k in range(1, count)]
    greet([{"head": other} for other in others])

    def attended_copy(k):
        owner = lax.rem(me + 1 + k, count)
        return pltpu.make_async_remote_copy(
            src_ref=att_out.at[owner],
            dst_ref=att_in.at[me],
            send_sem=att_sem.at[0, k],
            recv_sem=att_sem.at[1, k],
            device_id={"head": owner},
            device_id_type=pl.DeviceIdType.MESH,
        )

    def stores(slot, block):
        return [
            pltpu.make_async_copy(p_buf.at[slot], prob_ref.at[block], store_sem.at[0, slot]),
            pltpu.make_async_copy(g_buf.at[slot], slope_ref.at[block], store_sem.at[1, slot]),
        ]

    def step(t, carry):
        k, r = lax.div(t, per_owner), lax.rem(t, per_owner)
        owner = lax.rem(me + 1 + k, count)
        block = owner * per_owner + r
        slot = lax.rem(t, 2)

        @pl.when(t >= 2)
        def _():
            for copy in stores(slot, block):
                copy.wait()

        rows = pl.ds(pl.multiple_of(block * BLOCK, BLOCK), BLOCK)
        attended = forward_block(
            heads,
            slots,
            block,
            kb_ref,
            wt_ref,
            q_ref[rows, :],
            kv_ref,
            posc_ref[rows, :],
            posr_ref[block],
            p_buf.at[slot],
            g_buf.at[slot],
        )
        att_out[owner, pl.ds(pl.multiple_of(r * BLOCK, BLOCK), BLOCK), :] = attended
        for copy in stores(slot, block):
            copy.start()

        @pl.when((r == per_owner - 1) & (k < count - 1))
        def _():
            attended_copy(k).start()

        return carry

    lax.fori_loop(0, count * per_owner, step, 0)
    att_in[me] = att_out[me]
    for k in range(count - 1):
        attended_copy(k).wait()
    d_copies = []
    step_rows = 64
    half_rows = local_rows // 2
    for part in range(2):
        for start in range(part * half_rows, (part + 1) * half_rows, step_rows):
            rows = slice(start, start + step_rows)
            attended = jnp.concatenate([att_in[j, rows, :] for j in range(count)], axis=1)
            attended = attended.astype(jnp.float32)
            average = jnp.mean(attended, axis=1, keepdims=True)
            centered = attended - average
            variance = jnp.mean(centered * centered, axis=1, keepdims=True)
            inverse_std = lax.rsqrt(variance + epsilon)
            normed = centered * inverse_std
            gate = gate_ref[rows, :].astype(jnp.float32)
            normed_ref[rows, :] = normed
            gated_ref[rows, :] = (normed * gate).astype(jnp.bfloat16)
            d_normed = dg_ref[rows, :] * gate
            d_attended = inverse_std * (
                d_normed
                - jnp.mean(d_normed, axis=1, keepdims=True)
                - normed * jnp.mean(d_normed * normed, axis=1, keepdims=True)
            )
            d_attended = d_attended.astype(jnp.bfloat16)
            for j in range(count):
                d_out[j, rows, :] = d_attended[:, j * features : (j + 1) * features]
        rows = pl.ds(part * half_rows, half_rows)
        local = pltpu.make_async_copy(
            d_out.at[me, rows], d_heads_ref.at[me, rows], local_sem.at[part]
        )
        local.start()
        d_copies.append(local)
        for k, other in enumerate(others):
            d_copies.append(
                send(
                    d_out.at[other, rows],
                    d_heads_ref.at[me, rows],
                    d_sem.at[0, part, k],
                    d_sem.at[1, part, k],
                    {"head": other},
                )
            )
    mixed = jnp.dot(gated_ref[...], wout_ref[...], preferred_element_type=jnp.float32)
    mixed_ref[...] = (tok_ref[...].astype(jnp.float32) + mixed).astype(jnp.bfloat16)
    grad_u_ref[...] = (dg_ref[...] * normed_ref[...]).T.astype(jnp.bfloat16)
    for slot in range(2):
        for copy in stores(slot, me):
            copy.wait()
    for copy in d_copies:
        copy.wait()


def middle(key_blocks, weights, query, key_vals, positions_here, tokens, gate_u, d_gated, w_out):
    local_blocks, slots = key_blocks.shape
    local_rows, width = tokens.shape
    segment, features = query.shape
    heads = features // HEAD_DIM
    count = segment // local_rows
    exchanged = (count, local_rows, features)
    tall, wide = slots * BLOCK, heads * BLOCK
    anywhere = pl.BlockSpec(memory_space=pl.ANY)
    vmem = pl.BlockSpec(memory_space=pltpu.VMEM)
    smem = pl.BlockSpec(memory_space=pltpu.SMEM)
    stored = jax.ShapeDtypeStruct((local_blocks, tall, wide), jnp.bfloat16)
    return pl.pallas_call(
        functools.partial(middle_kernel, count, heads, slots),
        in_specs=[smem, smem] + [vmem] * 8,
        out_specs=[vmem, vmem, anywhere, anywhere, anywhere],
        out_shape=[
            jax.ShapeDtypeStruct(tokens.shape, jnp.bfloat16),
            jax.ShapeDtypeStruct((width, local_rows), jnp.bfloat16),
            jax.ShapeDtypeStruct(exchanged, jnp.bfloat16),
            stored,
            stored,
        ],
        scratch_shapes=[
            pltpu.VMEM((2, tall, wide), jnp.bfloat16),
            pltpu.VMEM((2, tall, wide), jnp.bfloat16),
            pltpu.VMEM(exchanged, jnp.bfloat16),
            pltpu.VMEM(exchanged, jnp.bfloat16),
            pltpu.VMEM(exchanged, jnp.bfloat16),
            pltpu.VMEM((local_rows, width), jnp.float32),
            pltpu.VMEM((local_rows, width), jnp.bfloat16),
            pltpu.SemaphoreType.DMA((2,)),
            pltpu.SemaphoreType.DMA((2, 2)),
            pltpu.SemaphoreType.DMA((2, count - 1)),
            pltpu.SemaphoreType.DMA((2, 2, count - 1)),
        ],
        compiler_params=pltpu.CompilerParams(
            collective_id=1, has_side_effects=True, vmem_limit_bytes=48 * 1024 * 1024
        ),
        name="middle",
    )(
        key_blocks.reshape(-1),
        weights.reshape(-1),
        query,
        key_vals.reshape(-1, BLOCK, 2 * features),
        positions_here.reshape(-1, 1),
        positions_here.reshape(local_blocks, 1, BLOCK),
        tokens,
        gate_u,
        d_gated,
        w_out,
    )


def distribute_kernel(
    count,
    features,
    tok_ref,
    w_ref,
    wout_ref,
    cot_ref,
    kv_out,
    q_out,
    gate_ref,
    dg_ref,
    w_buf,
    wout_buf,
    cot_buf,
    kv_buf,
    q_buf,
    w_sem,
    local_sem,
    kv_sem,
    q_sem,
    side_sem,
    core_sem,
    pass_sem,
):
    me, here = lax.axis_index("head"), lax.axis_index("blk")
    core, side = blk_partners(here)
    rows, width = tok_ref.shape
    lanes = 128
    per = lanes // features
    groups = count // per
    own_group, own_member = lax.div(me, per), lax.rem(me, per)

    def fetch(first, last, sem):
        columns = pl.ds(first * width, (last - first) * width)
        copy = pltpu.make_async_copy(w_ref.at[:, columns], w_buf.at[:, columns], sem)
        copy.start()
        return copy

    fetches = [fetch(2, 4, w_sem.at[0]), fetch(1, 2, w_sem.at[1]), fetch(0, 1, w_sem.at[2])]
    late = [
        pltpu.make_async_copy(wout_ref, wout_buf, w_sem.at[3]),
        pltpu.make_async_copy(cot_ref, cot_buf, w_sem.at[4]),
    ]
    for copy in late:
        copy.start()
    others = [lax.rem(me + k, count) for k in range(1, count)]
    greet([{"head": other} for other in others] + [{"blk": core}, {"blk": side}])

    def place(segment, source):
        start = pl.multiple_of((segment * count + source) * rows, rows)
        return kv_out.at[pl.ds(start, rows), :]

    def target(k, j):
        group = lax.rem(own_group + k, groups)
        return group * per + lax.rem(own_member + j, per)

    def source(k, j):
        group = lax.rem(own_group - k + groups, groups)
        return group * per + lax.rem(own_member - j + per, per)

    def silu_dot(weights):
        product = jnp.dot(tok_ref[...], weights, preferred_element_type=jnp.float32)
        half = 0.5 * product
        return (half + half * jnp.tanh(half)).astype(jnp.bfloat16)

    def columns_of(part, group):
        start = pl.multiple_of(part * width + group * lanes, lanes)
        return w_buf[:, pl.ds(start, lanes)]

    kv_copies, q_copies = [], []
    fetches[0].wait()
    for k in range(groups):
        group = lax.rem(own_group + k, groups)
        both = silu_dot(jnp.concatenate([columns_of(2, group), columns_of(3, group)], axis=1))
        for j in range(per):
            keys = both[:, j * features : (j + 1) * features]
            vals = both[:, lanes + j * features : lanes + (j + 1) * features]
            kv_buf[group * per + j] = jnp.concatenate([keys, vals], axis=1)
        for j in range(per):
            to, index = target(k, j), k * per + j
            if index == 0:
                local_kv = pltpu.make_async_copy(
                    kv_buf.at[me], place(here, me), local_sem.at[0]
                )
                local_kv.start()
                kv_copies.append(local_kv)
            else:
                kv_copies.append(
                    send(
                        kv_buf.at[to],
                        place(here, me),
                        kv_sem.at[0, index],
                        kv_sem.at[1, index],
                        {"head": to},
                    )
                )
    fetches[1].wait()
    for k in range(groups):
        group = lax.rem(own_group + k, groups)
        query = silu_dot(columns_of(1, group))
        for j in range(per):
            q_buf[group * per + j] = query[:, j * features : (j + 1) * features]
        for j in range(per):
            to, index = target(k, j), k * per + j
            if index == 0:
                local_q = pltpu.make_async_copy(q_buf.at[me], q_out.at[me], local_sem.at[1])
                local_q.start()
            else:
                q_copies.append(
                    send(
                        q_buf.at[to],
                        q_out.at[me],
                        q_sem.at[0, index],
                        q_sem.at[1, index],
                        {"head": to},
                    )
                )
    side_copies, core_copies, pass_copies = [], [], []
    lag = 2
    for index in range(count + lag):
        if index < count:
            if index == 0:
                local_kv.wait()
            else:
                kv_copies[index].wait_recv()
            chunk = place(here, source(index // per, index % per))
            side_copies.append(
                send(chunk, chunk, side_sem.at[0, index], side_sem.at[1, index], {"blk": side})
            )
            core_copies.append(
                send(chunk, chunk, core_sem.at[0, index], core_sem.at[1, index], {"blk": core})
            )
        if index == 1:
            fetches[2].wait()
            for c in range(0, width, 256):
                gate_ref[:, c : c + 256] = silu_dot(w_buf[:, c : c + 256])
        if index == 2:
            for copy in late:
                copy.wait()
            for c in range(0, width, 256):
                dg_ref[:, c : c + 256] = dot_nt(cot_buf[...], wout_buf[c : c + 256, :])
        j = index - lag
        if j >= 0:
            side_copies[j].wait_recv()
            chunk = place(side, source(j // per, j % per))
            pass_copies.append(
                send(chunk, chunk, pass_sem.at[0, j], pass_sem.at[1, j], {"blk": core})
            )
    local_q.wait()
    for copy in kv_copies[1:] + side_copies:
        copy.wait_send()
    for copy in q_copies + core_copies + pass_copies:
        copy.wait()


def distribute(tokens, w_proj, w_out, cotangent, count, groups):
    rows, width = tokens.shape
    features = width // count
    anywhere = pl.BlockSpec(memory_space=pl.ANY)
    vmem = pl.BlockSpec(memory_space=pltpu.VMEM)
    pair = pltpu.SemaphoreType.DMA((2, count))
    return pl.pallas_call(
        functools.partial(distribute_kernel, count, features),
        in_specs=[vmem, anywhere, anywhere, anywhere],
        out_specs=[anywhere, anywhere, vmem, vmem],
        out_shape=[
            jax.ShapeDtypeStruct((groups * count * rows, 2 * features), jnp.bfloat16),
            jax.ShapeDtypeStruct((count, rows, features), jnp.bfloat16),
            jax.ShapeDtypeStruct((rows, width), jnp.bfloat16),
            jax.ShapeDtypeStruct((rows, width), jnp.float32),
        ],
        scratch_shapes=[
            pltpu.VMEM(w_proj.shape, jnp.bfloat16),
            pltpu.VMEM(w_out.shape, jnp.bfloat16),
            pltpu.VMEM(cotangent.shape, jnp.bfloat16),
            pltpu.VMEM((count, rows, 2 * features), jnp.bfloat16),
            pltpu.VMEM((count, rows, features), jnp.bfloat16),
            pltpu.SemaphoreType.DMA((5,)),
            pltpu.SemaphoreType.DMA((2,)),
            pair,
            pair,
            pair,
            pair,
            pair,
        ],
        compiler_params=pltpu.CompilerParams(
            collective_id=0, has_side_effects=True, vmem_limit_bytes=48 * 1024 * 1024
        ),
        name="distribute",
    )(tokens, w_proj, w_out, cotangent)


def collect_kernel(
    chunks, part_ref, dq_ref, o_ref, core_in, side_out, side_in, near_sem, far_sem, side_sem
):
    here = lax.axis_index("blk")
    core, side = blk_partners(here)
    far = lax.rem(core + 2, 4)
    width, segment = dq_ref.shape
    rows = segment // chunks
    greet([{"blk": core}, {"blk": side}])
    far_copies = [
        send(
            part_ref.at[far, c], core_in.at[1, c], far_sem.at[0, c], far_sem.at[1, c], {"blk": core}
        )
        for c in range(chunks)
    ]
    near_copies = [
        send(
            part_ref.at[core, c],
            core_in.at[0, c],
            near_sem.at[0, c],
            near_sem.at[1, c],
            {"blk": core},
        )
        for c in range(chunks)
    ]
    side_copies = []
    for c in range(chunks):
        far_copies[c].wait_recv()
        total = part_ref[side, c].astype(jnp.float32) + core_in[1, c].astype(jnp.float32)
        side_out[c] = total.astype(jnp.bfloat16)
        side_copies.append(
            send(
                side_out.at[c], side_in.at[c], side_sem.at[0, c], side_sem.at[1, c], {"blk": side}
            )
        )
    o_ref[:width, :] = dq_ref[...]
    for c in range(chunks):
        near_copies[c].wait_recv()
        side_copies[c].wait_recv()
        total = (
            part_ref[here, c].astype(jnp.float32)
            + core_in[0, c].astype(jnp.float32)
            + side_in[c].astype(jnp.float32)
        )
        o_ref[width:, c * rows : (c + 1) * rows] = total.T
    for copy in far_copies + near_copies + side_copies:
        copy.wait_send()


def collect(partial, grad_query, groups):
    width, segment = grad_query.shape
    chunks = 8
    rows = segment // chunks
    vmem = pl.BlockSpec(memory_space=pltpu.VMEM)
    pair = pltpu.SemaphoreType.DMA((2, chunks))
    block = (chunks, rows, 2 * width)
    return pl.pallas_call(
        functools.partial(collect_kernel, chunks),
        in_specs=[vmem, vmem],
        out_specs=vmem,
        out_shape=jax.ShapeDtypeStruct((3 * width, segment), jnp.float32),
        scratch_shapes=[
            pltpu.VMEM((2,) + block, jnp.bfloat16),
            pltpu.VMEM(block, jnp.bfloat16),
            pltpu.VMEM(block, jnp.bfloat16),
            pair,
            pair,
            pair,
        ],
        compiler_params=pltpu.CompilerParams(
            collective_id=2, has_side_effects=True, vmem_limit_bytes=48 * 1024 * 1024
        ),
        name="collect",
    )(partial.reshape((groups,) + block), grad_query)


def shards(tokens, w_proj, w_out, cotangent, key_blocks, exposures, positions):
    head_count = lax.axis_size("head")
    group_count = lax.axis_size("blk")
    segment_index = lax.axis_index("blk")
    local_rows, width = tokens.shape
    features = width // head_count
    segment = local_rows * head_count
    key_all, query, gate_u, d_gated = distribute(
        tokens, w_proj, w_out, cotangent, head_count, group_count
    )
    query = query.reshape(segment, features)
    positions_here = lax.dynamic_slice_in_dim(positions, segment_index * segment, segment, 0)
    weights = jnp.log1p(exposures.astype(jnp.float32))
    mixed, grad_u, d_heads, prob, slope = middle(
        key_blocks, weights, query, key_all, positions_here, tokens, gate_u, d_gated, w_out
    )
    d_heads = d_heads.reshape(segment, features)
    grad_query, partial = attention_backward(
        key_blocks, query, d_heads, key_all, prob, slope
    )
    grad_qkv = collect(partial, grad_query, group_count).reshape(3, features, segment)
    return (mixed, grad_u, grad_qkv)


def solution(mesh):
    in_specs = (
        P(("blk", "head"), None),
        P(),
        P(),
        P(("blk", "head"), None),
        P("blk", None),
        P("blk", None),
        P(),
    )
    out_specs = (P(("blk", "head"), None), P(None, ("blk", "head")), P(None, "head", "blk"))
    return jax.shard_map(shards, mesh=mesh, in_specs=in_specs, out_specs=out_specs, check_vma=False)
```
